128 devices in a mesh: ent: 64 (over z, y, x_lo, core), rep: 2 (over x_hi).
Axes of the slice: x: 4 (x_hi: 2, x_lo: 2; x = x_hi * 2 + x_lo), y: 4, z: 4, core: 2. Of those that a mesh axis runs over, the one named last changes fastest.
Arguments:
- entity_table: bfloat16 [4, 65536, 768], P(None, 'ent'), may hold values from -6 to 6
- relation_table: bfloat16 [4, 1387, 768], replicated, may hold values from -16 to 24
- head_ids: int32 [4096], P(('rep', 'ent')), parts along dimension 0, may hold values from 0 to 65535, as said below
- relation_ids: int32 [4096], P(('rep', 'ent')), parts along dimension 0, may hold values from 0 to 1386
- order: int32 [4096], P(('rep', 'ent')), parts along dimension 0, may hold values from 0 to 2047, as said below
- tail_ids: int32 [4096], P(('rep', 'ent')), parts along dimension 0, may hold values from 0 to 65535
Outputs:
- ensemble_logprob: float32 [4096], P(('rep', 'ent')), parts along dimension 0
- member_logprob: float32 [4096, 4], P(('rep', 'ent')), parts along dimension 0
The draws below stay inside these ranges and needn't reach their ends.
There are 2 independent parts, one for each index of `rep`. The reference program is written for one: setup_inputs(seed, part) draws one part's arguments, and reference() takes and returns one part's arrays. A program takes and returns all parts, laid end to end along the dimension named above; an argument that names none is the same for every part. Nothing has to cross between parts.
Inputs may be any that keep to these rules, and one draw needn't show every extreme that they name: `head_ids`: the head of query row q lies in entities 1024 * (q // 32) to 1024 * (q // 32 + 1) - 1. `order`: a permutation of the query rows of the part that lists them by non-decreasing relation id, ties in row order.
All inputs are finite; a program needn't handle non-finite values.
Results may differ from the reference program's by a relative error of at most 0.00056.
Values may be sent and summed in bfloat16 or wider, within the bound.
A program may use at most 128 MiB of HBM per device.

```python
import jax
import jax.numpy as jnp
from jax import lax

MEMBERS = 4
D = 768
RELATIONS = 1387
E_DEV = 1024
Q_DEV = 32
ENTITIES = 65536
QUERIES = 2048
N_ENT = 64


def relation_pair(key):
    relation_vals = jax.random.randint(jax.random.fold_in(key, 11), (QUERIES,), 0, RELATIONS).astype(jnp.int32)
    sorted_rows = jnp.argsort(relation_vals, stable=True).astype(jnp.int32)
    return (relation_vals, sorted_rows)


def draw_relation_ids(key, part):
    return relation_pair(key)[0]


def draw_order(key, part):
    return relation_pair(key)[1]


def draw_head_ids(key, part):
    key = jax.random.fold_in(key, 3)
    row_index = jnp.arange(QUERIES, dtype=jnp.int32)
    owner = row_index // Q_DEV
    inside = jax.random.randint(key, (QUERIES,), 0, E_DEV).astype(jnp.int32)
    inside = jnp.where(row_index % Q_DEV == 0, 0, inside).astype(jnp.int32)
    return owner * E_DEV + inside


def draw_relation_table(key, part):
    key = jax.random.fold_in(key, 7)
    noise = jnp.clip(jax.random.normal(key, (MEMBERS, RELATIONS, D), jnp.float32), -4.0, 4.0)
    column = jnp.arange(D, dtype=jnp.int32)
    shift = jnp.where(column < D // 2, 8.0, 0.0).astype(jnp.float32)
    return (shift[None, None, :] + 4.0 * noise).astype(jnp.bfloat16)


def draw_entity_table(key, part):
    key = jax.random.fold_in(key, 5)
    key_base = jax.random.fold_in(key, 1)
    key_scale = jax.random.fold_in(key, 2)
    key_sign = jax.random.fold_in(key, 6)
    key_hot = jax.random.fold_in(key, 8)
    ramp = 1.0 + jnp.arange(ENTITIES, dtype=jnp.float32) / ENTITIES
    row_scale = 0.04 * jnp.exp(jax.random.uniform(key_scale, (MEMBERS, ENTITIES, 1), jnp.float32) * jnp.log(4.0))
    row_scale = row_scale * ramp[None, :, None]
    values = jax.random.normal(key_base, (MEMBERS, ENTITIES, D), jnp.float32)
    values = jnp.clip(values, -4.0, 4.0)
    drawn = values * row_scale
    direction = (2 * jax.random.randint(key_sign, (MEMBERS, 1, D), 0, 2) - 1).astype(jnp.float32)
    factor = jax.random.uniform(key_hot, (MEMBERS, ENTITIES, 1), jnp.float32, 1.0, 1.8)
    local_index = jnp.arange(ENTITIES, dtype=jnp.int32) % E_DEV
    hot_mask = jnp.where(local_index < 2, 1.0, 0.0).astype(jnp.float32)[None, :, None]
    strength = factor * jnp.sqrt(100.0 / (8.0 * D)) * hot_mask
    return (drawn + strength * direction).astype(jnp.bfloat16)


def set_ends(drawn, rng, smallest, high):
    dims = drawn.shape
    place = [jax.random.randint(jax.random.fold_in(rng, axis), (), 0, dims[axis]) for axis in range(len(dims))]
    drawn = drawn.at[tuple(place)].set(smallest)
    longest = dims.index(max(dims))
    place[longest] = (place[longest] + 1) % dims[longest]
    return drawn.at[tuple(place)].set(high)


def setup_inputs(seed: int = 0, part: int = 0) -> dict:
    streams_of = jax.random.split(jax.random.key(seed), 7)
    part_keys = jax.random.split(jax.random.fold_in(streams_of[6], part), 7)
    entity_table = draw_entity_table(jax.random.fold_in(streams_of[6], 71), part)
    relation_table = draw_relation_table(jax.random.fold_in(streams_of[6], 71), part)
    head_ids = draw_head_ids(jax.random.fold_in(jax.random.fold_in(streams_of[6], part), 71), part)
    relation_ids = draw_relation_ids(jax.random.fold_in(jax.random.fold_in(streams_of[6], part), 71), part)
    order = draw_order(jax.random.fold_in(jax.random.fold_in(streams_of[6], part), 71), part)
    tail_ids = set_ends(jax.random.randint(part_keys[5], (QUERIES,), 0, ENTITIES), jax.random.fold_in(part_keys[5], 1), 0, ENTITIES - 1).astype(jnp.int32)
    return {"entity_table": entity_table, "relation_table": relation_table, "head_ids": head_ids, "relation_ids": relation_ids, "order": order, "tail_ids": tail_ids}


def complex_product(left, right):
    half_width = left.shape[-1] // 2
    left_re, left_im = left[..., :half_width], left[..., half_width:]
    right_re, right_im = right[..., :half_width], right[..., half_width:]
    return jnp.concatenate([left_re * right_re - left_im * right_im, left_re * right_im + left_im * right_re], axis=-1)


def reference(entity_table, relation_table, head_ids, relation_ids, order, tail_ids):
    heads = entity_table[:, head_ids, :].astype(jnp.float32)
    relations = relation_table[:, relation_ids, :].astype(jnp.float32)
    query = complex_product(heads, relations).astype(jnp.bfloat16)
    member_rows = []
    for member in range(MEMBERS):
        query_m = query[member]
        blocks = entity_table[member].reshape(N_ENT, E_DEV, D)

        def step(carry, block):
            peak_now, total_now = carry
            scores = jnp.dot(query_m, block.T, preferred_element_type=jnp.float32)
            peak_new = jnp.maximum(peak_now, jnp.max(scores, axis=1))
            total_new = total_now * jnp.exp(peak_now - peak_new) + jnp.sum(jnp.exp(scores - peak_new[:, None]), axis=1)
            return (peak_new, total_new), None

        start = (jnp.full((QUERIES,), -jnp.inf, jnp.float32), jnp.zeros((QUERIES,), jnp.float32))
        (peak_all, total_all), _ = lax.scan(step, start, blocks)
        normalizer = peak_all + jnp.log(total_all)
        tail_rows = entity_table[member][tail_ids, :].astype(jnp.float32)
        tail_score = jnp.sum(query_m.astype(jnp.float32) * tail_rows, axis=1)
        member_rows.append(tail_score - normalizer)
    member_lp = jnp.stack(member_rows)
    member_logprob = jnp.take(member_lp, order, axis=1).T
    top_member = jnp.max(member_logprob, axis=1)
    ensemble_logprob = top_member + jnp.log(jnp.mean(jnp.exp(member_logprob - top_member[:, None]), axis=1))
    return ensemble_logprob, member_logprob
```

```python
import jax
import jax.numpy as jnp
from jax import lax
from jax.experimental import pallas as pl
from jax.experimental.pallas import tpu as pltpu
from jax.sharding import PartitionSpec as P

MESH = pl.DeviceIdType.MESH
F32 = jnp.float32
BF16 = jnp.bfloat16
CHUNK = 256


def complex_product(left, right):
    half_width = left.shape[-1] // 2
    left_re, left_im = (left[..., :half_width], left[..., half_width:])
    right_re, right_im = (right[..., :half_width], right[..., half_width:])
    return jnp.concatenate(
        [left_re * right_re - left_im * right_im, left_re * right_im + left_im * right_re], axis=-1
    )


PLAN = (("y", "z", True), ("z", "y", True), ("y", "z", False), ("z", "y", False))


def score_kernel(
    q_ref, tails_ref, order_ref, ent_ref, ens_ref, mem_ref,
    u, e, s0, s1, acc_m, acc_s, acc_t, tb, tv, stat, r, row, g,
    ring_send, ring_recv, x_send, x_recv, e_local, e_send, e_recv,
    t_send, t_recv, r_send, r_recv, g_send, g_recv,
):
    rows = e.shape[2]
    n_chunk = rows // CHUNK
    idx = lax.axis_index("ent")
    rep = lax.axis_index("rep")
    core = lax.rem(idx, 2)
    x = rep * 2 + lax.rem(idx // 2, 2)
    y = lax.rem(idx // 4, 4)
    z = idx // 16

    def dev(xx, yy, zz, cc):
        return {"ent": ((zz * 4 + yy) * 2 + lax.rem(xx, 2)) * 2 + cc, "rep": xx // 2}

    def wrap(v):
        return lax.rem(v + 4, 4)

    x_up, x_down = wrap(x + 1), wrap(x - 1)
    src = y * 4 + z

    for m in (2, 3, 0, 1):
        pltpu.make_async_copy(ent_ref.at[m], e.at[0, m], e_local.at[m]).start()
    for m in range(4):
        for k in range(2):
            u[m, k, y, z] = q_ref[m, 16 * k : 16 * k + 16, :]
    s1[...] = jnp.zeros_like(s1)
    acc_m[...] = jnp.zeros_like(acc_m)
    acc_s[...] = jnp.zeros_like(acc_s)
    acc_t[...] = jnp.zeros_like(acc_t)

    barrier = pltpu.get_barrier_semaphore()

    def greet(xx, cc, first):
        def step(i, carry):
            pl.semaphore_signal(
                barrier, inc=1, device_id=dev(xx, wrap(y + i // 4), wrap(z + lax.rem(i, 4)), cc), device_id_type=MESH
            )
            return carry

        lax.fori_loop(first, 16, step, 0)

    greet(x, core, 1)
    greet(x_up, core, 0)
    greet(x_down, core, 0)
    greet(x, 1 - core, 0)
    greet(rep * 2 + 1 - lax.rem(x, 2), 1 - core, 0)
    pl.semaphore_wait(barrier, 15 + 16 * 4)

    def ring_slice(m, ph, k, pos):
        axis = PLAN[m][ph]
        if ph == 0:
            return u.at[m, k, pos, z] if axis == "y" else u.at[m, k, y, pos]
        return u.at[m, k, pos] if axis == "y" else u.at[m, k, :, pos]

    def ring_copy(m, ph, k, j, offset, shift):
        axis = PLAN[m][ph]
        me = y if axis == "y" else z
        ref = ring_slice(m, ph, k, wrap(me + offset))
        to = dev(x, wrap(y + shift), z, core) if axis == "y" else dev(x, y, wrap(z + shift), core)
        return pltpu.make_async_remote_copy(
            src_ref=ref, dst_ref=ref, send_sem=ring_send.at[m, ph, k, j], recv_sem=ring_recv.at[m, ph, k, j],
            device_id=to, device_id_type=MESH,
        )

    def ring_start(m, ph, k):
        ring_copy(m, ph, k, 0, 0, 1).start()
        ring_copy(m, ph, k, 1, 0, -1).start()

    def ring_fwd(m, ph, k):
        if k % 2 == 0:
            ring_copy(m, ph, k, 0, -1, 1).wait_recv()
            ring_copy(m, ph, k, 2, -1, 1).start()
        else:
            ring_copy(m, ph, k, 1, 1, -1).wait_recv()
            ring_copy(m, ph, k, 2, 1, -1).start()

    def ring_fin(m, ph, k):
        if k % 2 == 0:
            ring_copy(m, ph, k, 1, 1, -1).wait_recv()
        else:
            ring_copy(m, ph, k, 0, -1, 1).wait_recv()
        ring_copy(m, ph, k, 2, 2, 1).wait_recv()

    def x_copy(m, k, i):
        axis = PLAN[m][1]
        offset = (0, -1, 1, 2)[i]
        pos = wrap((y if axis == "y" else z) + offset)
        a = u.at[m, k, pos] if axis == "y" else u.at[m, k, :, pos]
        b = u.at[m, k + 2, pos] if axis == "y" else u.at[m, k + 2, :, pos]
        return pltpu.make_async_remote_copy(
            src_ref=a, dst_ref=b, send_sem=x_send.at[m, i, k], recv_sem=x_recv.at[m, i, k],
            device_id=dev(x_up if k == 0 else x_down, y, z, core), device_id_type=MESH,
        )

    def e_copy(m):
        return pltpu.make_async_remote_copy(
            src_ref=ent_ref.at[m], dst_ref=e.at[1, m], send_sem=e_send.at[m], recv_sem=e_recv.at[m],
            device_id=dev(x, y, z, 1 - core), device_id_type=MESH,
        )

    for m in (2, 3):
        for k in range(2):
            ring_start(m, 0, k)
    for m in (0, 1):
        for k in range(2):
            ring_start(m, 0, k)
    for m in (2, 3, 0, 1):
        e_copy(m).start()

    pltpu.make_async_copy(tails_ref, tb.at[src, pl.ds(0, 2)], t_recv.at[0]).start()

    def tail_copy(n, xx, yy, zz):
        a, b = ((0, 2), (0, 1), (1, 1))[n], ((0, 2), (2, 1), (3, 1))[n]
        return pltpu.make_async_remote_copy(
            src_ref=tails_ref.at[pl.ds(*a)], dst_ref=tb.at[src, pl.ds(*b)], send_sem=t_send.at[n],
            recv_sem=t_recv.at[n], device_id=dev(xx, yy, zz, core), device_id_type=MESH,
        )

    def send_all(copy, n, xx, first):
        def step(i, carry):
            copy(n, xx, wrap(y + i // 4), wrap(z + lax.rem(i, 4))).start()
            return carry

        lax.fori_loop(first, 16, step, 0)

    send_all(tail_copy, 0, x, 1)
    send_all(tail_copy, 1, x_up, 0)
    send_all(tail_copy, 2, x_down, 0)

    for m in (2, 3):
        for k in range(2):
            ring_fwd(m, 0, k)
    for m in (2, 3):
        for k in range(2):
            ring_fin(m, 0, k)
            ring_start(m, 1, k)
            x_copy(m, k, 0).start()
    for m in (0, 1):
        for k in range(2):
            ring_fwd(m, 0, k)
    for m in (0, 1):
        for k in range(2):
            ring_fin(m, 0, k)
            x_copy(m, k, 0).start()
            ring_start(m, 1, k)

    for n, part in enumerate((tb.at[:, pl.ds(0, 2)], tb.at[:, pl.ds(2, 1)], tb.at[:, pl.ds(3, 1)])):
        pltpu.make_async_copy(part, part, t_recv.at[n]).wait()
    group = lax.broadcasted_iota(jnp.int32, (8, 128), 1) // 16
    for k in range(4):
        for half in range(2):
            lanes = jnp.zeros((8, 128), jnp.int32)
            for i in range(8):
                lanes = jnp.where(group == i, tb[half * 8 + i, k], lanes)
            tv[k, :, half * 128 : half * 128 + 128] = lanes

    def fwd_second(m, k):
        ring_fwd(m, 1, k)
        if m >= 2:
            x_copy(m, k, 1 if k == 0 else 2).start()

    def fin_second(m, k):
        ring_fin(m, 1, k)
        if m >= 2:
            x_copy(m, k, 2 if k == 0 else 1).start()
            x_copy(m, k, 3).start()

    def x_started(m, k):
        x_copy(m, k - 2, 0).wait_recv()
        ring_start(m, 1, k)

    def x_done(m, k):
        for i in range(4):
            x_copy(m, k - 2, i).wait_recv()

    for k in range(2):
        for m in (2, 3):
            fwd_second(m, k)

    def batch_of(t):
        first = t < 8
        m = jnp.where(first, lax.rem(t, 2) + jnp.where(t < 4, 2, 0), lax.rem(t, 4))
        k = jnp.where(first, lax.rem(t // 2, 2), 2 + (t - 8) // 4)
        return m, k

    def e_ready(m):
        pltpu.make_async_copy(ent_ref.at[m], e.at[0, m], e_local.at[m]).wait()
        e_copy(m).wait_recv()

    def stat_copy(n, xx, yy, zz):
        ks = ((0, 2), (2, 1), (3, 1))[n]
        return pltpu.make_async_remote_copy(
            src_ref=stat.at[yy // 2, pl.ds(*ks)], dst_ref=r.at[src, pl.ds(*ks)], send_sem=r_send.at[n],
            recv_sem=r_recv.at[n], device_id=dev(xx, yy, zz, core), device_id_type=MESH,
        )

    def comm(t):
        if t == 0:
            fin_second(2, 0)
            e_ready(2)
        if t == 1:
            fin_second(3, 0)
            e_ready(3)
            x_started(0, 2)
            x_started(1, 2)
        if t == 2:
            fin_second(2, 1)
            x_started(0, 3)
            x_started(1, 3)
        if t == 3:
            fin_second(3, 1)
            fwd_second(0, 0)
            fwd_second(1, 0)
        if t == 4:
            fwd_second(0, 1)
            fwd_second(1, 1)
            fin_second(0, 0)
            e_ready(0)
        if t == 5:
            fin_second(1, 0)
            e_ready(1)
        if t == 6:
            fwd_second(0, 2)
            fwd_second(1, 2)
            fin_second(0, 1)
        if t == 7:
            fin_second(1, 1)
        if t == 8:
            fwd_second(0, 3)
            fwd_second(1, 3)
            fin_second(0, 2)
        if t == 9:
            fin_second(1, 2)
            pltpu.make_async_copy(stat.at[y // 2, pl.ds(0, 2)], r.at[src, pl.ds(0, 2)], r_recv.at[0]).start()
            send_all(stat_copy, 0, x, 1)
        if t == 10:
            x_done(2, 2)
        if t == 11:
            x_done(3, 2)
        if t == 12:
            fin_second(0, 3)
        if t == 13:
            fin_second(1, 3)
            send_all(stat_copy, 1, x_down, 0)
        if t == 14:
            x_done(2, 3)
        if t == 15:
            x_done(3, 3)

    sub = lax.broadcasted_iota(jnp.int32, (8, 256), 0)

    def dot(out, m, k, c):
        j, cc = c // n_chunk, lax.rem(c, n_chunk)
        left = e[j, m, pl.ds(pl.multiple_of(cc * CHUNK, CHUNK), CHUNK), :]
        right = u[m, k].reshape(256, e.shape[3])
        out[...] = lax.dot_general(left, right, (((1,), (1,)), ((), ())), preferred_element_type=F32)

    def process(ref, k, c, fresh):
        j = c // n_chunk
        base = (idx + j * (1 - 2 * core)) * rows + lax.rem(c, n_chunk) * CHUNK
        rel = tv[k] - base - sub
        old = jnp.where(fresh, -jnp.inf, acc_m[...])
        blocks = CHUNK // 8
        tops = [ref[8 * i : 8 * i + 8, :] for i in range(4)]
        for i in range(4, blocks):
            tops[i % 4] = jnp.maximum(tops[i % 4], ref[8 * i : 8 * i + 8, :])
        top = jnp.maximum(jnp.maximum(tops[0], tops[1]), jnp.maximum(tops[2], tops[3]))
        new = jnp.maximum(old, top)
        total = jnp.where(fresh, 0.0, acc_s[...]) * jnp.exp(old - new)
        sums = [total, jnp.zeros_like(total)]
        tail = jnp.where(fresh, 0.0, acc_t[...])
        for i in range(blocks):
            v = ref[8 * i : 8 * i + 8, :]
            sums[i % 2] = sums[i % 2] + jnp.exp(v - new)
            tail = jnp.where(rel == 8 * i, v, tail)
        acc_m[...] = new
        acc_s[...] = sums[0] + sums[1]
        acc_t[...] = tail

    def finish(m, k):
        top = jnp.max(acc_m[...], axis=0, keepdims=True)
        total = jnp.sum(acc_s[...] * jnp.exp(acc_m[...] - top), axis=0, keepdims=True)
        lse = top + jnp.log(total)
        tail = jnp.sum(acc_t[...], axis=0, keepdims=True)
        for half in range(2):
            cols = slice(half * 128, half * 128 + 128)
            stat[half, k, pl.ds(m, 1), :] = lse[:, cols]
            stat[half, k, pl.ds(m + 4, 1), :] = tail[:, cols]

    last = 2 * n_chunk - 1

    def batch(t, carry):
        for j in range(16):
            pl.when(t == j)(lambda j=j: comm(j))
        m, k = batch_of(t)
        m_old, k_old = batch_of(jnp.maximum(t - 1, 0))

        def pair(i, carry):
            head = i == 0
            dot(s0, m, k, 2 * i)
            process(s1, jnp.where(head, k_old, k), jnp.where(head, last, 2 * i - 1), False)

            @pl.when(jnp.logical_and(head, t > 0))
            def _():
                finish(m_old, k_old)

            dot(s1, m, k, 2 * i + 1)
            process(s0, k, 2 * i, head)
            return carry

        lax.fori_loop(0, n_chunk, pair, 0)
        return carry

    lax.fori_loop(0, 16, batch, 0)
    process(s1, 3, last, False)
    finish(3, 3)
    send_all(stat_copy, 2, x_up, 0)

    for n, part in enumerate((r.at[:, pl.ds(0, 2)], r.at[:, pl.ds(2, 1)], r.at[:, pl.ds(3, 1)])):
        pltpu.make_async_copy(part, part, r_recv.at[n]).wait()
    lane = lax.broadcasted_iota(jnp.int32, (1, 128), 1)
    begin = (lax.rem(y, 2) * 4 + z) * 16
    packed = jnp.zeros((1, 128), F32)
    for h in range(2):
        tiles = [r[i, h] for i in range(16)] + [r[i, h + 2] for i in range(16)]
        top = tiles[0]
        tails = tiles[0]
        for tile in tiles[1:]:
            top = jnp.maximum(top, tile)
            tails = tails + tile
        total = jnp.zeros_like(top)
        for tile in tiles:
            total = total + jnp.exp(tile - top)
        value = tails[4:8, :] - (top + jnp.log(total))[0:4, :]
        value = jnp.concatenate([value, value], axis=0)
        value = pltpu.roll(value, lax.rem(128 - begin, 128), 1)
        for m in range(4):
            at = m * 32 + h * 16
            moved = value[m : m + 1, :] if at == 0 else pltpu.roll(value, at, 1)[m : m + 1, :]
            packed = jnp.where(jnp.logical_and(lane >= at, lane < at + 16), moved, packed)
    row[...] = packed

    pltpu.make_async_copy(row, g.at[idx], g_recv.at[0]).start()

    def g_step(i, carry):
        pltpu.make_async_remote_copy(
            src_ref=row, dst_ref=g.at[idx], send_sem=g_send.at[0], recv_sem=g_recv.at[0],
            device_id={"ent": lax.rem(idx + i, 64), "rep": rep}, device_id_type=MESH,
        ).start()
        return carry

    lax.fori_loop(1, 64, g_step, 0)
    pltpu.make_async_copy(g, g, g_recv.at[0]).wait()

    order = order_ref[...]
    owner = order // 32
    inside = order - owner * 32
    picked = jnp.zeros(order.shape, F32)
    for i in range(64):
        picked = jnp.where(owner == i, g[i], picked)
    lane32 = lax.broadcasted_iota(jnp.int32, order.shape, 1)
    cols = []
    for m in range(4):
        col = jnp.sum(jnp.where(lane32 == inside + m * 32, picked, 0.0), axis=1, keepdims=True)
        mem_ref[:, m : m + 1] = col
        cols.append(col)
    best = jnp.maximum(jnp.maximum(cols[0], cols[1]), jnp.maximum(cols[2], cols[3]))
    mean = sum(jnp.exp(c - best) for c in cols) * 0.25
    ens_ref[...] = best + jnp.log(mean)

    for m in range(4):
        for k in range(2):
            for j in range(3):
                ring_copy(m, 0, k, j, 0, 1).wait_send()
        for k in range(4 if PLAN[m][2] else 2):
            for j in range(3):
                ring_copy(m, 1, k, j, 0, 1).wait_send()
        for k in range(2):
            for i in range(1 if PLAN[m][2] else 4):
                x_copy(m, k, i).wait_send()
        e_copy(m).wait_send()
    for n, part in enumerate((tb.at[pl.ds(0, 15), pl.ds(0, 2)], tb.at[:, pl.ds(2, 1)], tb.at[:, pl.ds(3, 1)])):
        pltpu.make_async_copy(part, part, t_send.at[n]).wait()
    for n, part in enumerate((r.at[pl.ds(0, 15), pl.ds(0, 2)], r.at[:, pl.ds(2, 1)], r.at[:, pl.ds(3, 1)])):
        pltpu.make_async_copy(part, part, r_send.at[n]).wait()
    part = g.at[pl.ds(0, 63)]
    pltpu.make_async_copy(part, part, g_send.at[0]).wait()


def per_device(entity_table, relation_table, head_ids, relation_ids, order, tail_ids):
    members, local_count, width = entity_table.shape
    offset = lax.axis_index("ent") * local_count
    entity_index = jnp.arange(local_count, dtype=jnp.int32)
    head_picker = ((head_ids - offset)[:, None] == entity_index[None, :]).astype(BF16)
    heads = jnp.einsum("qe,med->mqd", head_picker, entity_table, preferred_element_type=F32)
    table_rows = relation_table.shape[1]
    picker = (relation_ids[:, None] == jnp.arange(table_rows, dtype=jnp.int32)[None, :]).astype(BF16)
    relations = jnp.einsum("qr,mrd->mqd", picker, relation_table, preferred_element_type=F32)
    query = complex_product(heads, relations).astype(BF16)
    tails = jnp.tile(tail_ids.reshape(2, 1, 16), (1, 1, 8))
    order_wide = jnp.broadcast_to(order[:, None], (32, 128))
    vmem = pl.BlockSpec(memory_space=pltpu.VMEM)
    dma = pltpu.SemaphoreType.DMA
    ens, mem = pl.pallas_call(
        score_kernel,
        out_shape=(jax.ShapeDtypeStruct((32, 1), F32), jax.ShapeDtypeStruct((32, 4), F32)),
        in_specs=[vmem, vmem, vmem, pl.BlockSpec(memory_space=pl.ANY)],
        out_specs=(vmem, vmem),
        scratch_shapes=[
            pltpu.VMEM((4, 4, 4, 4, 16, width), BF16),
            pltpu.VMEM((2, 4, local_count, width), BF16),
            pltpu.VMEM((CHUNK, 256), F32),
            pltpu.VMEM((CHUNK, 256), F32),
            pltpu.VMEM((8, 256), F32),
            pltpu.VMEM((8, 256), F32),
            pltpu.VMEM((8, 256), F32),
            pltpu.VMEM((16, 4, 1, 128), jnp.int32),
            pltpu.VMEM((4, 8, 256), jnp.int32),
            pltpu.VMEM((2, 4, 8, 128), F32),
            pltpu.VMEM((16, 4, 8, 128), F32),
            pltpu.VMEM((1, 128), F32),
            pltpu.VMEM((64, 1, 128), F32),
            dma((4, 2, 4, 3)),
            dma((4, 2, 4, 3)),
            dma((4, 4, 2)),
            dma((4, 4, 2)),
            dma((4,)),
            dma((4,)),
            dma((4,)),
            dma((3,)),
            dma((3,)),
            dma((3,)),
            dma((3,)),
            dma((1,)),
            dma((1,)),
        ],
        compiler_params=pltpu.CompilerParams(
            collective_id=0, has_side_effects=True, vmem_limit_bytes=40 * 1024 * 1024
        ),
        cost_estimate=pl.CostEstimate(
            flops=2 * members * 2048 * local_count * width,
            bytes_accessed=4 * members * local_count * width,
            transcendentals=members * 2048 * local_count,
        ),
        name="score_exchange",
    )(query, tails, order_wide, entity_table)
    return (ens.reshape(32), mem)


def solution(mesh):
    placed = (
        P(None, "ent", None),
        P(),
        P(("rep", "ent")),
        P(("rep", "ent")),
        P(("rep", "ent")),
        P(("rep", "ent")),
    )
    return jax.shard_map(
        per_device,
        mesh=mesh,
        in_specs=placed,
        out_specs=(P(("rep", "ent")), P(("rep", "ent"), None)),
        check_vma=False,
    )
```

```python
import jax
import jax.numpy as jnp
from jax import lax
from jax.experimental import pallas as pl
from jax.experimental.pallas import tpu as pltpu
from jax.sharding import PartitionSpec as P

MESH = pl.DeviceIdType.MESH
F32 = jnp.float32
BF16 = jnp.bfloat16


def complex_product(left, right):
    half_width = left.shape[-1] // 2
    left_re, left_im = (left[..., :half_width], left[..., half_width:])
    right_re, right_im = (right[..., :half_width], right[..., half_width:])
    return jnp.concatenate(
        [left_re * right_re - left_im * right_im, left_re * right_im + left_im * right_re], axis=-1
    )


PLAN = (("y", "z", True), ("z", "y", True), ("y", "z", False), ("z", "y", False))


def score_kernel(
    q_ref, tails_ref, order_ref, ent_ref, ens_ref, mem_ref,
    u, e, s0, s1, tb, tv, stat, rx, rz, ry, g,
    ring_send, ring_recv, x_send, x_recv, e_local, e_send, e_recv,
    t_send, t_recv, stat_send, stat_recv,
):
    rows = e.shape[2]
    idx = lax.axis_index("ent")
    rep = lax.axis_index("rep")
    core = lax.rem(idx, 2)
    x_lo = lax.rem(idx // 2, 2)
    x = rep * 2 + x_lo
    y = lax.rem(idx // 4, 4)
    z = idx // 16

    def dev(xx, yy, zz, cc):
        return {"ent": ((zz * 4 + yy) * 2 + lax.rem(xx, 2)) * 2 + cc, "rep": xx // 2}

    def wrap(v):
        return lax.rem(v + 4, 4)

    def along(axis, shift):
        if axis == "x":
            return dev(wrap(x + shift), y, z, core)
        return dev(x, wrap(y + shift), z, core) if axis == "y" else dev(x, y, wrap(z + shift), core)

    pair = rep * 2 + 1 - x_lo
    others = (dev(pair, y, z, core), dev(x, y, z, 1 - core), dev(pair, y, z, 1 - core))

    def remote(src, dst, send_sem, recv_sem, to):
        return pltpu.make_async_remote_copy(
            src_ref=src, dst_ref=dst, send_sem=send_sem, recv_sem=recv_sem, device_id=to, device_id_type=MESH
        )

    barrier = pltpu.get_barrier_semaphore()
    partners = [along(axis, shift) for axis in "zy" for shift in (1, 2, 3)]
    partners += [along("x", 1), along("x", -1), others[1], others[2]]
    for partner in partners:
        pl.semaphore_signal(barrier, inc=1, device_id=partner, device_id_type=MESH)

    for m in (2, 3, 0, 1):
        pltpu.make_async_copy(ent_ref.at[m], e.at[0, m], e_local.at[m]).start()
    for m in range(4):
        for k in range(2):
            u[m, k, y, z] = q_ref[m, 16 * k : 16 * k + 16, :]
    for k in range(2):
        tb[k, y, z] = tails_ref[k]
    pl.semaphore_wait(barrier, len(partners))

    def ring_slice(m, ph, k, pos):
        axis = PLAN[m][ph]
        if ph == 0:
            return u.at[m, k, pos, z] if axis == "y" else u.at[m, k, y, pos]
        return u.at[m, k, pos] if axis == "y" else u.at[m, k, :, pos]

    def ring_copy(m, ph, k, j, offset, shift):
        axis = PLAN[m][ph]
        ref = ring_slice(m, ph, k, wrap((y if axis == "y" else z) + offset))
        return remote(ref, ref, ring_send.at[m, ph, k, j], ring_recv.at[m, ph, k, j], along(axis, shift))

    def ring_start(m, ph, k):
        ring_copy(m, ph, k, 0, 0, 1).start()
        ring_copy(m, ph, k, 1, 0, -1).start()

    def ring_fwd(m, ph, k):
        if k % 2 == 0:
            ring_copy(m, ph, k, 0, -1, 1).wait_recv()
            ring_copy(m, ph, k, 2, -1, 1).start()
        else:
            ring_copy(m, ph, k, 1, 1, -1).wait_recv()
            ring_copy(m, ph, k, 2, 1, -1).start()

    def ring_fin(m, ph, k):
        if k % 2 == 0:
            ring_copy(m, ph, k, 1, 1, -1).wait_recv()
        else:
            ring_copy(m, ph, k, 0, -1, 1).wait_recv()
        ring_copy(m, ph, k, 2, 2, 1).wait_recv()

    def x_copy(m, k, i):
        axis = PLAN[m][1]
        pos = wrap((y if axis == "y" else z) + (0, -1, 1, 2)[i])
        a = u.at[m, k, pos] if axis == "y" else u.at[m, k, :, pos]
        b = u.at[m, k + 2, pos] if axis == "y" else u.at[m, k + 2, :, pos]
        return remote(a, b, x_send.at[m, i, k], x_recv.at[m, i, k], along("x", 1 if k == 0 else -1))

    def e_copy(m):
        return remote(ent_ref.at[m], e.at[1, m], e_send.at[m], e_recv.at[m], others[1])

    def tail_copy(ph, j, offset, shift):
        ref = tb.at[pl.ds(0, 2), wrap(y + offset), z] if ph == 0 else tb.at[pl.ds(0, 2), :, wrap(z + offset)]
        return remote(ref, ref, t_send.at[ph, j], t_recv.at[ph, j], along("yz"[ph], shift))

    def tail_x(k):
        return remote(tb.at[k], tb.at[k + 2], t_send.at[2, k], t_recv.at[2, k], along("x", 1 if k == 0 else -1))

    def tail_start(ph):
        tail_copy(ph, 0, 0, 1).start()
        tail_copy(ph, 1, 0, -1).start()

    def tail_fwd(ph):
        tail_copy(ph, 0, -1, 1).wait_recv()
        tail_copy(ph, 2, -1, 1).start()

    def tail_fin(ph):
        tail_copy(ph, 1, 1, -1).wait_recv()
        tail_copy(ph, 2, 2, 1).wait_recv()

    for m in (2, 3):
        for k in range(2):
            ring_start(m, 0, k)
    tail_start(0)
    for m in (0, 1):
        for k in range(2):
            ring_start(m, 0, k)
    for m in (2, 3, 0, 1):
        e_copy(m).start()
    for m in (2, 3):
        for k in range(2):
            ring_fwd(m, 0, k)
    tail_fwd(0)
    for k in range(2):
        for m in (2, 3):
            ring_fin(m, 0, k)
            ring_start(m, 1, k)
            x_copy(m, k, 0).start()
    tail_fin(0)
    tail_start(1)
    for m in (0, 1):
        for k in range(2):
            ring_fwd(m, 0, k)
    for k in range(2):
        for m in (0, 1):
            ring_fin(m, 0, k)
            x_copy(m, k, 0).start()
            ring_start(m, 1, k)
    tail_fwd(1)

    def fwd_second(m, k):
        ring_fwd(m, 1, k)
        if m >= 2:
            x_copy(m, k, 1 if k == 0 else 2).start()

    def fin_second(m, k):
        ring_fin(m, 1, k)
        if m >= 2:
            x_copy(m, k, 2 if k == 0 else 1).start()
            x_copy(m, k, 3).start()

    def x_started(m, k):
        x_copy(m, k - 2, 0).wait_recv()
        ring_start(m, 1, k)

    def x_done(m, k):
        for i in range(4):
            x_copy(m, k - 2, i).wait_recv()

    for k in range(2):
        for m in (2, 3):
            fwd_second(m, k)
    tail_fin(1)
    for k in range(2):
        tail_x(k).start()
    for k in range(2):
        tail_x(k).wait_recv()
    group = lax.broadcasted_iota(jnp.int32, (8, 128), 1) // 16
    for k in range(4):
        for half in range(2):
            lanes = jnp.zeros((8, 128), jnp.int32)
            for i in range(8):
                lanes = jnp.where(group == i, tb[k, half * 2 + i // 4, i % 4], lanes)
            tv[k, :, half * 128 : half * 128 + 128] = lanes

    def batch_of(t):
        first = t < 8
        m = jnp.where(first, lax.rem(t, 2) + jnp.where(t < 4, 2, 0), lax.rem(t, 4))
        k = jnp.where(first, lax.rem(t // 2, 2), 2 + (t - 8) // 4)
        return m, k

    def e_ready(m):
        pltpu.make_async_copy(ent_ref.at[m], e.at[0, m], e_local.at[m]).wait()
        e_copy(m).wait_recv()

    def stat_x(k):
        return remote(
            stat.at[k + 2], rx.at[k], stat_send.at[0, k], stat_recv.at[0, k], along("x", -1 if k == 0 else 1)
        )

    def comm(t):
        if t == 0:
            fin_second(2, 0)
            e_ready(2)
        if t == 1:
            fin_second(3, 0)
            e_ready(3)
            x_started(0, 2)
            x_started(1, 2)
        if t == 2:
            fin_second(2, 1)
            x_started(0, 3)
            x_started(1, 3)
        if t == 3:
            fin_second(3, 1)
            fwd_second(0, 0)
            fwd_second(1, 0)
        if t == 4:
            fwd_second(0, 1)
            fwd_second(1, 1)
            fin_second(0, 0)
            e_ready(0)
        if t == 5:
            fin_second(1, 0)
            e_ready(1)
        if t == 6:
            fwd_second(0, 2)
            fwd_second(1, 2)
            fin_second(0, 1)
        if t == 7:
            fin_second(1, 1)
        if t == 8:
            fwd_second(0, 3)
            fwd_second(1, 3)
            fin_second(0, 2)
        if t == 9:
            fin_second(1, 2)
        if t == 10:
            x_done(2, 2)
        if t == 11:
            x_done(3, 2)
        if t == 12:
            fin_second(0, 3)
        if t == 13:
            fin_second(1, 3)
            stat_x(0).start()
        if t == 14:
            x_done(2, 3)
        if t == 15:
            x_done(3, 3)

    sub = lax.broadcasted_iota(jnp.int32, (8, 256), 0)
    blocks = rows // 8

    def dot(out, m, k):
        right = u[m, k].reshape(256, e.shape[3])
        for j in range(2):
            out[j * rows : j * rows + rows, :] = lax.dot_general(
                e[j, m], right, (((1,), (1,)), ((), ())), preferred_element_type=F32
            )

    def process(ref, m, k):
        rel = [tv[k] - (idx + j * (1 - 2 * core)) * rows - sub for j in range(2)]
        tops = [ref[8 * i : 8 * i + 8, :] for i in range(4)]
        for i in range(4, 2 * blocks):
            tops[i % 4] = jnp.maximum(tops[i % 4], ref[8 * i : 8 * i + 8, :])
        top = jnp.maximum(jnp.maximum(tops[0], tops[1]), jnp.maximum(tops[2], tops[3]))
        top = jnp.max(top, axis=0, keepdims=True)
        wide = jnp.broadcast_to(top, (8, 256))
        sums = [jnp.zeros((8, 256), F32)] * 4
        tails = [jnp.zeros((8, 256), F32)] * 2
        for i in range(2 * blocks):
            v = ref[8 * i : 8 * i + 8, :]
            sums[i % 4] = sums[i % 4] + jnp.exp(v - wide)
            j = i // blocks
            tails[j] = jnp.where(rel[j] == 8 * (i % blocks), v, tails[j])
        total = jnp.sum((sums[0] + sums[1]) + (sums[2] + sums[3]), axis=0, keepdims=True)
        lse = top + jnp.log(total)
        tail = jnp.sum(tails[0] + tails[1], axis=0, keepdims=True)
        for half in range(2):
            cols = slice(half * 128, half * 128 + 128)
            stat[k, half, pl.ds(m, 1), :] = lse[:, cols]
            stat[k, half, pl.ds(m + 4, 1), :] = tail[:, cols]

    s1[...] = jnp.zeros_like(s1)

    def batches(i, carry):
        for p in range(2):
            t = 2 * i + p
            for j in range(p, 16, 2):
                pl.when(i == j // 2)(lambda j=j: comm(j))
            m, k = batch_of(t)
            m_old, k_old = batch_of(jnp.maximum(t - 1, 0))
            dot((s0, s1)[p], m, k)
            process((s1, s0)[p], m_old, k_old)
        return carry

    lax.fori_loop(0, 8, batches, 0)
    process(s1, 3, 3)

    stat_x(1).start()
    is_lse = lax.broadcasted_iota(jnp.int32, (8, 128), 0) < 4

    def merge(tiles):
        top = tiles[0]
        total = tiles[0]
        for tile in tiles[1:]:
            top = jnp.maximum(top, tile)
            total = total + tile
        mass = jnp.exp(tiles[0] - top)
        for tile in tiles[1:]:
            mass = mass + jnp.exp(tile - top)
        return jnp.where(is_lse, top + jnp.log(mass), total)

    def stat_ring(buf, n, axis, o):
        return remote(buf.at[0], buf.at[o], stat_send.at[n, o - 1], stat_recv.at[n, o - 1], along(axis, o))

    for h in range(2):
        stat_x(h).wait_recv()
        for half in range(2):
            rz[0, h, half] = merge([stat[h, half], rx[h, half]])
    for o in (2, 1, 3):
        stat_ring(rz, 1, "z", o).start()
    for o in (1, 3, 2):
        stat_ring(rz, 1, "z", o).wait_recv()
    for h in range(2):
        for half in range(2):
            ry[0, h, half] = merge([rz[o, h, half] for o in range(4)])
    for o in (2, 1, 3):
        stat_ring(ry, 2, "y", o).start()
    for o in (1, 3, 2):
        stat_ring(ry, 2, "y", o).wait_recv()
    mine = x_lo * 2 + core
    for half in range(2):
        both = [merge([ry[o, h, half] for o in range(4)]) for h in range(2)]
        g[mine, half] = jnp.concatenate([v[4:8, :] - v[0:4, :] for v in both], axis=0)

    def g_copy(n):
        return remote(g.at[mine], g.at[mine], stat_send.at[3, n], stat_recv.at[3, n], others[n])

    for n in range(3):
        g_copy(n).start()
    order = order_ref[...]
    d = order // 32
    h = lax.rem(order // 16, 2)
    dy = lax.rem(d // 4, 4)
    lane_at = (lax.rem(dy, 2) * 4 + d // 16) * 16 + lax.rem(order, 16)
    tile_at = (lax.rem(d, 4) * 2 + dy // 2) * 2 + h
    lane = lax.broadcasted_iota(jnp.int32, order.shape, 1)
    for n in range(3):
        g_copy(n).wait_recv()
    picked = [jnp.zeros(order.shape, F32)] * 4
    for p in range(4):
        for half in range(2):
            tile = g[p, half]
            for hh in range(2):
                hit = tile_at == (p * 2 + half) * 2 + hh
                for m in range(4):
                    picked[m] = jnp.where(hit, tile[hh * 4 + m : hh * 4 + m + 1, :], picked[m])
    cols = []
    for m in range(4):
        col = jnp.sum(jnp.where(lane == lane_at, picked[m], 0.0), axis=1, keepdims=True)
        mem_ref[:, m : m + 1] = col
        cols.append(col)
    best = jnp.maximum(jnp.maximum(cols[0], cols[1]), jnp.maximum(cols[2], cols[3]))
    mean = sum(jnp.exp(c - best) for c in cols) * 0.25
    ens_ref[...] = best + jnp.log(mean)

    for m in range(4):
        for k in range(2):
            for j in range(3):
                ring_copy(m, 0, k, j, 0, 1).wait_send()
        for k in range(4 if PLAN[m][2] else 2):
            for j in range(3):
                ring_copy(m, 1, k, j, 0, 1).wait_send()
        for k in range(2):
            for i in range(1 if PLAN[m][2] else 4):
                x_copy(m, k, i).wait_send()
        e_copy(m).wait_send()
    for j in range(3):
        tail_copy(0, j, 0, 1).wait_send()
        tail_copy(1, j, 0, 1).wait_send()
        stat_ring(rz, 1, "z", j + 1).wait_send()
        stat_ring(ry, 2, "y", j + 1).wait_send()
        g_copy(j).wait_send()
    for k in range(2):
        tail_x(k).wait_send()
        stat_x(k).wait_send()


def per_device(entity_table, relation_table, head_ids, relation_ids, order, tail_ids):
    members, local_count, width = entity_table.shape
    offset = lax.axis_index("ent") * local_count
    entity_index = jnp.arange(local_count, dtype=jnp.int32)
    head_picker = ((head_ids - offset)[:, None] == entity_index[None, :]).astype(BF16)
    heads = jnp.einsum("qe,med->mqd", head_picker, entity_table, preferred_element_type=F32)
    table_rows = relation_table.shape[1]
    picker = (relation_ids[:, None] == jnp.arange(table_rows, dtype=jnp.int32)[None, :]).astype(BF16)
    relations = jnp.einsum("qr,mrd->mqd", picker, relation_table, preferred_element_type=F32)
    query = complex_product(heads, relations).astype(BF16)
    tails = jnp.tile(tail_ids.reshape(2, 1, 16), (1, 1, 8))
    order_wide = jnp.broadcast_to(order[:, None], (32, 128))
    vmem = pl.BlockSpec(memory_space=pltpu.VMEM)
    dma = pltpu.SemaphoreType.DMA
    ens, mem = pl.pallas_call(
        score_kernel,
        out_shape=(jax.ShapeDtypeStruct((32, 1), F32), jax.ShapeDtypeStruct((32, 4), F32)),
        in_specs=[vmem, vmem, vmem, pl.BlockSpec(memory_space=pl.ANY)],
        out_specs=(vmem, vmem),
        scratch_shapes=[
            pltpu.VMEM((4, 4, 4, 4, 16, width), BF16),
            pltpu.VMEM((2, 4, local_count, width), BF16),
            pltpu.VMEM((2 * local_count, 256), F32),
            pltpu.VMEM((2 * local_count, 256), F32),
            pltpu.VMEM((4, 4, 4, 1, 128), jnp.int32),
            pltpu.VMEM((4, 8, 256), jnp.int32),
            pltpu.VMEM((4, 2, 8, 128), F32),
            pltpu.VMEM((2, 2, 8, 128), F32),
            pltpu.VMEM((4, 2, 2, 8, 128), F32),
            pltpu.VMEM((4, 2, 2, 8, 128), F32),
            pltpu.VMEM((4, 2, 8, 128), F32),
            dma((4, 2, 4, 3)),
            dma((4, 2, 4, 3)),
            dma((4, 4, 2)),
            dma((4, 4, 2)),
            dma((4,)),
            dma((4,)),
            dma((4,)),
            dma((3, 3)),
            dma((3, 3)),
            dma((4, 3)),
            dma((4, 3)),
        ],
        compiler_params=pltpu.CompilerParams(
            collective_id=0, has_side_effects=True, vmem_limit_bytes=58 * 1024 * 1024
        ),
        cost_estimate=pl.CostEstimate(
            flops=2 * members * 2048 * local_count * width,
            bytes_accessed=4 * members * local_count * width,
            transcendentals=members * 2048 * local_count,
        ),
        name="score_exchange",
    )(query, tails, order_wide, entity_table)
    return (ens.reshape(32), mem)


def solution(mesh):
    placed = (
        P(None, "ent", None),
        P(),
        P(("rep", "ent")),
        P(("rep", "ent")),
        P(("rep", "ent")),
        P(("rep", "ent")),
    )
    return jax.shard_map(
        per_device,
        mesh=mesh,
        in_specs=placed,
        out_specs=(P(("rep", "ent")), P(("rep", "ent"), None)),
        check_vma=False,
    )
```

```python
import jax
import jax.numpy as jnp
from jax import lax
from jax.experimental import pallas as pl
from jax.experimental.pallas import tpu as pltpu
from jax.sharding import PartitionSpec as P

MESH = pl.DeviceIdType.MESH
F32 = jnp.float32
BF16 = jnp.bfloat16

AXES = ("yz", "zy", "yz", "zy")
BATCH_M = (2, 3, 2, 3, 0, 1, 0, 1, 2, 2, 0, 1, 0, 1, 3, 3)
BATCH_K = (0, 0, 1, 1, 0, 0, 1, 1, 2, 3, 2, 2, 3, 3, 2, 3)
N_MSG = 160


def lookup(table, t):
    low = sum(v << (2 * i) for i, v in enumerate(table[:8]))
    high = sum(v << (2 * i) for i, v in enumerate(table[8:]))
    return (jnp.where(t < 8, low, high) >> (2 * lax.rem(t, 8))) & 3


def score_kernel(
    q_ref, tails_ref, order_ref, ent_ref, ens_ref, mem_ref,
    u, e, s0, s1, tb, tv, stat, r, row, g,
    send, recv, e_local, e_send, e_recv, r_send, r_recv, g_send, g_recv,
):
    rows, width = e.shape[2:]
    idx = lax.axis_index("ent")
    rep = lax.axis_index("rep")
    core = lax.rem(idx, 2)
    x_lo = lax.rem(idx // 2, 2)
    x = rep * 2 + x_lo
    y = lax.rem(idx // 4, 4)
    z = idx // 16
    src = y * 4 + z

    def dev(xx, yy, zz, cc):
        return {"ent": ((zz * 4 + yy) * 2 + lax.rem(xx, 2)) * 2 + cc, "rep": xx // 2}

    def wrap(v):
        return lax.rem(v + 4, 4)

    def along(axis, shift):
        if axis == "x":
            return dev(wrap(x + shift), y, z, core)
        return dev(x, wrap(y + shift), z, core) if axis == "y" else dev(x, y, wrap(z + shift), core)

    def remote(a, b, send_sem, recv_sem, to):
        return pltpu.make_async_remote_copy(
            src_ref=a, dst_ref=b, send_sem=send_sem, recv_sem=recv_sem, device_id=to, device_id_type=MESH
        )

    def e_own(m):
        return pltpu.make_async_copy(ent_ref.at[m], e.at[0, m], e_local.at[m])

    def e_copy(m):
        return remote(ent_ref.at[m], e.at[1, m], e_send.at[m], e_recv.at[m], dev(x, y, z, 1 - core))

    for m in (2, 3, 0, 1):
        e_own(m).start()

    barrier = pltpu.get_barrier_semaphore()
    partners = [along(axis, shift) for axis in "xyz" for shift in (1, -1)] + [dev(x, y, z, 1 - core)]
    for partner in partners:
        pl.semaphore_signal(barrier, inc=1, device_id=partner, device_id_type=MESH)

    for m in range(4):
        for k in range(2):
            u[m, k, y, z] = q_ref[m, 16 * k : 16 * k + 16, :]
    for k in range(2):
        tb[k, y, z] = tails_ref[k]
    pl.semaphore_wait(barrier, len(partners))

    numbers = {}
    sent = {}

    def sem_of(key):
        return numbers.setdefault(key, len(numbers))

    def at(m, k, first, second):
        return u.at[m, k, first, second] if AXES[m][0] == "y" else u.at[m, k, second, first]

    def own(m, ph):
        return y if AXES[m][ph] == "y" else z

    def piece(m, q):
        return slice(None) if q is None else wrap(own(m, 0) + q)

    def ring(m, ph, k, q, j):
        offset, shift = ((0, 1), (0, -1), (-1, 1) if k % 2 == 0 else (1, -1))[j]
        pos = wrap(own(m, ph) + offset)
        ref = at(m, k, pos, own(m, 1)) if ph == 0 else at(m, k, piece(m, q), pos)
        n = sem_of((m, ph, k, q, j))
        return remote(ref, ref, send.at[n], recv.at[n], along(AXES[m][ph], shift))

    def cross(m, k, q, i):
        pos = wrap(own(m, 1) + i)
        n = sem_of((m, k, q, i))
        return remote(
            at(m, k, piece(m, q), pos), at(m, k + 2, piece(m, q), pos), send.at[n], recv.at[n],
            along("x", 1 if k == 0 else -1),
        )

    def tail_ring(ph, j):
        offset, shift = ((0, 1), (0, -1), (-1, 1))[j]
        ref = tb.at[pl.ds(0, 2), wrap(y + offset), z] if ph == 0 else tb.at[pl.ds(0, 2), :, wrap(z + offset)]
        n = sem_of(("tail", ph, j))
        return remote(ref, ref, send.at[n], recv.at[n], along("yz"[ph], shift))

    def tail_cross(k):
        n = sem_of(("tail", k))
        return remote(tb.at[k], tb.at[k + 2], send.at[n], recv.at[n], along("x", 1 if k == 0 else -1))

    def start(make, *args):
        make(*args).start()
        sent[(make, args)] = True

    def arrived(make, *args):
        make(*args).wait_recv()

    def ring_start(m, ph, k, q=None):
        start(ring, m, ph, k, q, 0)
        start(ring, m, ph, k, q, 1)

    def ring_fwd(m, ph, k, q=None):
        arrived(ring, m, ph, k, q, k % 2)
        start(ring, m, ph, k, q, 2)

    def ring_fin(m, ph, k, q=None):
        arrived(ring, m, ph, k, q, 1 - k % 2)
        arrived(ring, m, ph, k, q, 2)

    for m in (2, 3, 0, 1):
        if m == 0:
            for j in range(2):
                start(tail_ring, 0, j)
        for k in range(2):
            ring_start(m, 0, k)
        for k in range(2):
            if m >= 2:
                ring_start(m, 1, k, 0)
            start(cross, m, k, 0, 0)
    for m in (2, 3, 0, 1):
        e_copy(m).start()

    def second(m, k, q):
        if m >= 2:
            ring_start(m, 1, k, q)
        start(cross, m, k, q, 0)

    for m in (2, 3, 0, 1):
        for k in range(2):
            ring_fwd(m, 0, k)
            second(m, k, -1 if k == 0 else 1)
        for k in range(2):
            arrived(ring, m, 0, k, None, 1 - k)
            second(m, k, 1 if k == 0 else -1)
    arrived(tail_ring, 0, 0)
    start(tail_ring, 0, 2)
    for m in (2, 3):
        for k in range(2):
            ring_fwd(m, 1, k, 0)
    for m in (2, 3, 0, 1):
        for k in range(2):
            arrived(ring, m, 0, k, None, 2)
            second(m, k, 2)
    arrived(tail_ring, 0, 1)
    arrived(tail_ring, 0, 2)
    for j in range(2):
        start(tail_ring, 1, j)
    for k in range(2):
        for m in (2, 3):
            ring_fwd(m, 1, k, -1)
            ring_fwd(m, 1, k, 1)
    for k in range(2):
        for m in (0, 1):
            ring_start(m, 1, k)
    arrived(tail_ring, 1, 0)
    start(tail_ring, 1, 2)
    for k in range(2):
        for m in (2, 3):
            ring_fwd(m, 1, k, 2)
    arrived(tail_ring, 1, 1)
    arrived(tail_ring, 1, 2)
    for k in range(2):
        start(tail_cross, k)

    def second_done(m, k):
        for q in (0, -1, 1, 2):
            ring_fin(m, 1, k, q)
        for i in (-1, 1, 2):
            start(cross, m, k, None, i)

    def crossed(m, k):
        for q in (0, -1, 1, 2):
            arrived(cross, m, k - 2, q, 0)
        if m >= 2:
            for i in (-1, 1, 2):
                arrived(cross, m, k - 2, None, i)
        else:
            ring_start(m, 1, k)

    def e_ready(m):
        e_own(m).wait()
        e_copy(m).wait_recv()

    def stat_copy(n, xx, yy, zz):
        ks = ((0, 2), (2, 1), (3, 1))[n]
        return remote(
            stat.at[yy // 2, pl.ds(*ks)], r.at[src, pl.ds(*ks)], r_send.at[n], r_recv.at[n], dev(xx, yy, zz, core)
        )

    def send_all(n, xx, first):
        def step(i, carry):
            stat_copy(n, xx, wrap(y + i // 4), wrap(z + lax.rem(i, 4))).start()
            return carry

        lax.fori_loop(first, 16, step, 0)

    def comm(t):
        if t == 0:
            second_done(2, 0)
            e_ready(2)
        if t == 1:
            second_done(3, 0)
            e_ready(3)
            for k in range(2):
                arrived(tail_cross, k)
            group = lax.broadcasted_iota(jnp.int32, (8, 128), 1) // 16
            for k in range(4):
                for half in range(2):
                    lanes = jnp.zeros((8, 128), jnp.int32)
                    for i in range(8):
                        lanes = jnp.where(group == i, tb[k, half * 2 + i // 4, i % 4], lanes)
                    tv[k, :, half * 128 : half * 128 + 128] = lanes
        if t == 2:
            second_done(2, 1)
            ring_fwd(0, 1, 0)
            ring_fwd(1, 1, 0)
        if t == 3:
            second_done(3, 1)
            ring_fwd(0, 1, 1)
            ring_fwd(1, 1, 1)
        if t == 4:
            e_ready(0)
            crossed(0, 2)
            crossed(1, 2)
            ring_fin(0, 1, 0)
        if t == 5:
            e_ready(1)
            crossed(0, 3)
            crossed(1, 3)
            ring_fin(1, 1, 0)
        if t == 6:
            ring_fin(0, 1, 1)
        if t == 7:
            ring_fin(1, 1, 1)
            ring_fwd(0, 1, 2)
            ring_fwd(1, 1, 2)
        if t == 8:
            crossed(2, 2)
        if t == 9:
            ring_fwd(0, 1, 3)
            ring_fwd(1, 1, 3)
            crossed(2, 3)
        if t == 10:
            pltpu.make_async_copy(stat.at[y // 2, pl.ds(0, 2)], r.at[src, pl.ds(0, 2)], r_recv.at[0]).start()
            send_all(0, x, 1)
            ring_fin(0, 1, 2)
        if t == 11:
            ring_fin(1, 1, 2)
        if t == 12:
            ring_fin(0, 1, 3)
        if t == 13:
            ring_fin(1, 1, 3)
        if t == 14:
            crossed(3, 2)
        if t == 15:
            crossed(3, 3)

    sub = lax.broadcasted_iota(jnp.int32, (8, 256), 0)
    blocks = rows // 8

    def dot(out, m, k):
        right = u[m, k].reshape(256, width)
        for j in range(2):
            out[j * rows : j * rows + rows, :] = lax.dot_general(
                e[j, m], right, (((1,), (1,)), ((), ())), preferred_element_type=F32
            )

    def process(ref, m, k):
        rel = [tv[k] - (idx + j * (1 - 2 * core)) * rows - sub for j in range(2)]
        tops = [ref[8 * i : 8 * i + 8, :] for i in range(4)]
        for i in range(4, 2 * blocks):
            tops[i % 4] = jnp.maximum(tops[i % 4], ref[8 * i : 8 * i + 8, :])
        top = jnp.maximum(jnp.maximum(tops[0], tops[1]), jnp.maximum(tops[2], tops[3]))
        top = jnp.max(top, axis=0, keepdims=True)
        wide = jnp.broadcast_to(top, (8, 256))
        sums = [jnp.zeros((8, 256), F32)] * 4
        true = [jnp.zeros((8, 256), F32)] * 2
        for i in range(2 * blocks):
            v = ref[8 * i : 8 * i + 8, :]
            sums[i % 4] = sums[i % 4] + jnp.exp(v - wide)
            j = i // blocks
            true[j] = jnp.where(rel[j] == 8 * (i % blocks), v, true[j])
        total = jnp.sum((sums[0] + sums[1]) + (sums[2] + sums[3]), axis=0, keepdims=True)
        lse = top + jnp.log(total)
        tail = jnp.sum(true[0] + true[1], axis=0, keepdims=True)
        for half in range(2):
            cols = slice(half * 128, half * 128 + 128)
            stat[half, k, pl.ds(m, 1), :] = lse[:, cols]
            stat[half, k, pl.ds(m + 4, 1), :] = tail[:, cols]

    s1[...] = jnp.zeros_like(s1)
    tv[...] = jnp.zeros_like(tv)

    def batches(i, carry):
        for p in range(2):
            t = 2 * i + p
            for j in range(p, 16, 2):
                pl.when(i == j // 2)(lambda j=j: comm(j))
            old = jnp.maximum(t - 1, 0)
            dot((s0, s1)[p], lookup(BATCH_M, t), lookup(BATCH_K, t))
            process((s1, s0)[p], lookup(BATCH_M, old), lookup(BATCH_K, old))
        return carry

    lax.fori_loop(0, 8, batches, 0)
    send_all(1, wrap(x - 1), 0)
    process(s1, BATCH_M[15], BATCH_K[15])
    send_all(2, wrap(x + 1), 0)

    whole = (r.at[:, pl.ds(0, 2)], r.at[:, pl.ds(2, 1)], r.at[:, pl.ds(3, 1)])
    part = r.at[pl.ds(0, 15), pl.ds(0, 2)]
    pltpu.make_async_copy(whole[0], whole[0], r_recv.at[0]).wait()
    pltpu.make_async_copy(part, part, r_send.at[0]).wait()

    def reduce(k):
        tiles = [r[i, k] for i in range(16)]
        top = tiles[0]
        total = tiles[0]
        for tile in tiles[1:]:
            top = jnp.maximum(top, tile)
            total = total + tile
        mass = jnp.exp(tiles[0] - top)
        for tile in tiles[1:]:
            mass = mass + jnp.exp(tile - top)
        return top, mass, total

    near = [reduce(0), reduce(1)]
    for copies in list(sent):
        make, args = copies
        make(*args).wait_send()
    for m in range(4):
        e_copy(m).wait_send()
    lane = lax.broadcasted_iota(jnp.int32, (1, 128), 1)
    begin = (lax.rem(y, 2) * 4 + z) * 16
    packed = jnp.zeros((1, 128), F32)
    for h in range(2):
        pltpu.make_async_copy(whole[1 + h], whole[1 + h], r_recv.at[1 + h]).wait()
        top0, mass0, total0 = near[h]
        top1, mass1, total1 = reduce(h + 2)
        top = jnp.maximum(top0, top1)
        lse = top + jnp.log(mass0 * jnp.exp(top0 - top) + mass1 * jnp.exp(top1 - top))
        value = (total0 + total1)[4:8, :] - lse[0:4, :]
        value = jnp.concatenate([value, value], axis=0)
        value = pltpu.roll(value, lax.rem(128 - begin, 128), 1)
        for m in range(4):
            to = m * 32 + h * 16
            moved = value[m : m + 1, :] if to == 0 else pltpu.roll(value, to, 1)[m : m + 1, :]
            packed = jnp.where(jnp.logical_and(lane >= to, lane < to + 16), moved, packed)
    row[...] = packed

    pltpu.make_async_copy(row, g.at[idx], g_recv.at[0]).start()

    def g_step(i, carry):
        to = {"ent": lax.rem(idx + i, 64), "rep": rep}
        remote(row, g.at[idx], g_send.at[0], g_recv.at[0], to).start()
        return carry

    lax.fori_loop(1, 64, g_step, 0)
    order = order_ref[...]
    sub32 = lax.broadcasted_iota(jnp.int32, order.shape, 0)
    owner = order // 32
    inside = order - owner * 32
    lane32 = lax.broadcasted_iota(jnp.int32, order.shape, 1)
    for n in range(2):
        pltpu.make_async_copy(whole[1 + n], whole[1 + n], r_send.at[1 + n]).wait()
    part = g.at[pl.ds(0, 63)]
    pltpu.make_async_copy(part, part, g_send.at[0]).wait()
    pltpu.make_async_copy(g, g, g_recv.at[0]).wait()

    picked = jnp.zeros(order.shape, F32)
    for i in range(64):
        picked = jnp.where(owner == i, g[i], picked)
    cols = []
    for m in range(4):
        col = jnp.sum(jnp.where(lane32 == inside + m * 32, picked, 0.0), axis=1, keepdims=True)
        cols.append(col)
    best = jnp.maximum(jnp.maximum(cols[0], cols[1]), jnp.maximum(cols[2], cols[3]))
    mean = sum(jnp.exp(c - best) for c in cols) * 0.25
    diagonal = sub32 == lane32
    for m, col in enumerate(cols + [best + jnp.log(mean)]):
        line = jnp.sum(jnp.where(diagonal, col, 0.0), axis=0, keepdims=True)[:, :32]
        if m < 4:
            mem_ref[m : m + 1, :] = line
        else:
            ens_ref[...] = line


def build_kernel(
    head_ref, rel_ref, order_ref, tail_ref, ent_ref, table_ref, q_ref, tails_ref, wide_ref,
    head_rows, rel_rows, qf, sem,
):
    rows, width = ent_ref.shape[1:]
    half_width = width // 2
    offset = lax.axis_index("ent") * rows

    def fetch(i, carry):
        head = pl.multiple_of((head_ref[i] - offset) // 16 * 16, 16)
        pltpu.make_async_copy(ent_ref.at[:, pl.ds(head, 16)], head_rows.at[i], sem.at[0]).start()
        pltpu.make_async_copy(table_ref.at[rel_ref[i]], rel_rows.at[i], sem.at[1]).start()
        return carry

    lax.fori_loop(0, 32, fetch, 0, unroll=4)
    lane16 = lax.rem(lax.broadcasted_iota(jnp.int32, (1, 128), 1), 16)
    for k in range(2):
        acc = jnp.zeros((1, 128), jnp.int32)
        for i in range(16):
            acc = jnp.where(lane16 == i, tail_ref[k * 16 + i], acc)
        tails_ref[k] = acc
    for i in range(32):
        wide_ref[i : i + 1, :] = jnp.full((1, 128), order_ref[i], jnp.int32)
    pltpu.make_async_copy(rel_rows, rel_rows, sem.at[1]).wait()
    pltpu.make_async_copy(head_rows, head_rows, sem.at[0]).wait()
    sub16 = lax.broadcasted_iota(jnp.int32, (16, width), 0)

    def pick(i, carry):
        hit = sub16 == lax.rem(head_ref[i], 16)
        right = rel_rows[i].astype(F32)
        for m in range(4):
            left = jnp.sum(jnp.where(hit, head_rows[i, m].astype(F32), 0.0), axis=0, keepdims=True)
            a, b = left[:, :half_width], left[:, half_width:]
            c, d = right[m : m + 1, :half_width], right[m : m + 1, half_width:]
            qf[m, pl.ds(i, 1), :half_width] = a * c - b * d
            qf[m, pl.ds(i, 1), half_width:] = a * d + b * c
        return carry

    lax.fori_loop(0, 32, pick, 0, unroll=4)
    q_ref[...] = qf[...].astype(BF16)


def per_device(entity_table, relation_table, head_ids, relation_ids, order, tail_ids):
    members, local_count, width = entity_table.shape
    vmem = pl.BlockSpec(memory_space=pltpu.VMEM)
    smem = pl.BlockSpec(memory_space=pltpu.SMEM)
    hbm = pl.BlockSpec(memory_space=pl.ANY)
    dma = pltpu.SemaphoreType.DMA
    query, tails, order_wide = pl.pallas_call(
        build_kernel,
        out_shape=(
            jax.ShapeDtypeStruct((members, 32, width), BF16),
            jax.ShapeDtypeStruct((2, 1, 128), jnp.int32),
            jax.ShapeDtypeStruct((32, 128), jnp.int32),
        ),
        in_specs=[smem, smem, smem, smem, hbm, hbm],
        out_specs=(vmem, vmem, vmem),
        scratch_shapes=[
            pltpu.VMEM((32, members, 16, width), BF16),
            pltpu.VMEM((32, members, width), BF16),
            pltpu.VMEM((members, 32, width), F32),
            dma((2,)),
        ],
        compiler_params=pltpu.CompilerParams(vmem_limit_bytes=58 * 1024 * 1024),
        name="build_queries",
    )(head_ids, relation_ids, order, tail_ids, entity_table, jnp.transpose(relation_table, (1, 0, 2)))
    ens, mem = pl.pallas_call(
        score_kernel,
        out_shape=(jax.ShapeDtypeStruct((1, 32), F32), jax.ShapeDtypeStruct((4, 32), F32)),
        in_specs=[vmem, vmem, vmem, hbm],
        out_specs=(vmem, vmem),
        scratch_shapes=[
            pltpu.VMEM((4, 4, 4, 4, 16, width), BF16),
            pltpu.VMEM((2, 4, local_count, width), BF16),
            pltpu.VMEM((2 * local_count, 256), F32),
            pltpu.VMEM((2 * local_count, 256), F32),
            pltpu.VMEM((4, 4, 4, 1, 128), jnp.int32),
            pltpu.VMEM((4, 8, 256), jnp.int32),
            pltpu.VMEM((2, 4, 8, 128), F32),
            pltpu.VMEM((16, 4, 8, 128), F32),
            pltpu.VMEM((1, 128), F32),
            pltpu.VMEM((64, 1, 128), F32),
            dma((N_MSG,)),
            dma((N_MSG,)),
            dma((4,)),
            dma((4,)),
            dma((4,)),
            dma((3,)),
            dma((3,)),
            dma((1,)),
            dma((1,)),
        ],
        compiler_params=pltpu.CompilerParams(
            collective_id=0, has_side_effects=True, vmem_limit_bytes=58 * 1024 * 1024
        ),
        cost_estimate=pl.CostEstimate(
            flops=2 * members * 2048 * local_count * width,
            bytes_accessed=4 * members * local_count * width,
            transcendentals=members * 2048 * local_count,
        ),
        name="score_exchange",
    )(query, tails, order_wide, entity_table)
    return (ens.reshape(32), mem.T)


def solution(mesh):
    placed = (
        P(None, "ent", None),
        P(),
        P(("rep", "ent")),
        P(("rep", "ent")),
        P(("rep", "ent")),
        P(("rep", "ent")),
    )
    return jax.shard_map(
        per_device,
        mesh=mesh,
        in_specs=placed,
        out_specs=(P(("rep", "ent")), P(("rep", "ent"), None)),
        check_vma=False,
    )
```

```python
import jax
import jax.numpy as jnp
from jax import lax
from jax.experimental import pallas as pl
from jax.experimental.pallas import tpu as pltpu
from jax.sharding import PartitionSpec as P

MESH = pl.DeviceIdType.MESH
F32 = jnp.float32
BF16 = jnp.bfloat16

AXES = ("yz", "zy", "yz", "zy")
BATCH_M = (2, 3, 2, 3, 0, 1, 0, 1, 2, 2, 0, 1, 0, 1, 3, 3)
BATCH_K = (0, 0, 1, 1, 0, 0, 1, 1, 2, 3, 2, 2, 3, 3, 2, 3)
N_MSG = 160


def lookup(table, t):
    low = sum(v << (2 * i) for i, v in enumerate(table[:8]))
    high = sum(v << (2 * i) for i, v in enumerate(table[8:]))
    return (jnp.where(t < 8, low, high) >> (2 * lax.rem(t, 8))) & 3


def score_kernel(
    q_ref, tails_ref, order_ref, ent_ref, out_ref,
    u, e, s0, s1, tb, tv, stat, rowed, r, row, g,
    send, recv, e_local, e_send, e_recv, r_send, r_recv, g_send, g_recv,
):
    rows, width = e.shape[2:]
    idx = lax.axis_index("ent")
    rep = lax.axis_index("rep")
    core = lax.rem(idx, 2)
    x_lo = lax.rem(idx // 2, 2)
    x = rep * 2 + x_lo
    y = lax.rem(idx // 4, 4)
    z = idx // 16
    src = y * 4 + z

    def dev(xx, yy, zz, cc):
        return {"ent": ((zz * 4 + yy) * 2 + lax.rem(xx, 2)) * 2 + cc, "rep": xx // 2}

    def wrap(v):
        return lax.rem(v + 4, 4)

    def along(axis, shift):
        if axis == "x":
            return dev(wrap(x + shift), y, z, core)
        return dev(x, wrap(y + shift), z, core) if axis == "y" else dev(x, y, wrap(z + shift), core)

    def remote(a, b, send_sem, recv_sem, to):
        return pltpu.make_async_remote_copy(
            src_ref=a, dst_ref=b, send_sem=send_sem, recv_sem=recv_sem, device_id=to, device_id_type=MESH
        )

    def e_own(m):
        return pltpu.make_async_copy(ent_ref.at[m], e.at[0, m], e_local.at[m])

    def e_copy(m):
        return remote(ent_ref.at[m], e.at[1, m], e_send.at[m], e_recv.at[m], dev(x, y, z, 1 - core))

    for m in (2, 3, 0, 1):
        e_own(m).start()

    barrier = pltpu.get_barrier_semaphore()
    partners = [along(axis, shift) for axis in "xyz" for shift in (1, -1)] + [dev(x, y, z, 1 - core)]
    for partner in partners:
        pl.semaphore_signal(barrier, inc=1, device_id=partner, device_id_type=MESH)

    for m in range(4):
        for k in range(2):
            u[m, k, y, z] = q_ref[m, 16 * k : 16 * k + 16, :]
    for k in range(2):
        tb[k, y, z] = tails_ref[k]
    pl.semaphore_wait(barrier, len(partners))

    numbers = {}
    sent = {}

    def sem_of(key):
        return numbers.setdefault(key, len(numbers))

    def at(m, k, first, second):
        return u.at[m, k, first, second] if AXES[m][0] == "y" else u.at[m, k, second, first]

    def own(m, ph):
        return y if AXES[m][ph] == "y" else z

    def piece(m, q):
        return slice(None) if q is None else wrap(own(m, 0) + q)

    def ring(m, ph, k, q, j):
        offset, shift = ((0, 1), (0, -1), (-1, 1) if k % 2 == 0 else (1, -1))[j]
        pos = wrap(own(m, ph) + offset)
        ref = at(m, k, pos, own(m, 1)) if ph == 0 else at(m, k, piece(m, q), pos)
        n = sem_of((m, ph, k, q, j))
        return remote(ref, ref, send.at[n], recv.at[n], along(AXES[m][ph], shift))

    def cross(m, k, q, i):
        pos = wrap(own(m, 1) + i)
        n = sem_of((m, k, q, i))
        return remote(
            at(m, k, piece(m, q), pos), at(m, k + 2, piece(m, q), pos), send.at[n], recv.at[n],
            along("x", 1 if k == 0 else -1),
        )

    def tail_ring(ph, j):
        offset, shift = ((0, 1), (0, -1), (-1, 1))[j]
        ref = tb.at[pl.ds(0, 2), wrap(y + offset), z] if ph == 0 else tb.at[pl.ds(0, 2), :, wrap(z + offset)]
        n = sem_of(("tail", ph, j))
        return remote(ref, ref, send.at[n], recv.at[n], along("yz"[ph], shift))

    def tail_cross(k):
        n = sem_of(("tail", k))
        return remote(tb.at[k], tb.at[k + 2], send.at[n], recv.at[n], along("x", 1 if k == 0 else -1))

    def start(make, *args):
        make(*args).start()
        sent[(make, args)] = True

    def arrived(make, *args):
        make(*args).wait_recv()

    def ring_start(m, ph, k, q=None):
        start(ring, m, ph, k, q, 0)
        start(ring, m, ph, k, q, 1)

    def ring_fwd(m, ph, k, q=None):
        arrived(ring, m, ph, k, q, k % 2)
        start(ring, m, ph, k, q, 2)

    def ring_fin(m, ph, k, q=None):
        arrived(ring, m, ph, k, q, 1 - k % 2)
        arrived(ring, m, ph, k, q, 2)

    for m in (2, 3, 0, 1):
        if m == 0:
            for j in range(2):
                start(tail_ring, 0, j)
        for k in range(2):
            ring_start(m, 0, k)
        for k in range(2):
            if m >= 2:
                ring_start(m, 1, k, 0)
            start(cross, m, k, 0, 0)
    for m in (2, 3, 0, 1):
        e_copy(m).start()

    def second(m, k, q):
        if m >= 2:
            ring_start(m, 1, k, q)
        start(cross, m, k, q, 0)

    for m in (2, 3, 0, 1):
        for k in range(2):
            ring_fwd(m, 0, k)
            second(m, k, -1 if k == 0 else 1)
        for k in range(2):
            arrived(ring, m, 0, k, None, 1 - k)
            second(m, k, 1 if k == 0 else -1)
    arrived(tail_ring, 0, 0)
    start(tail_ring, 0, 2)
    for m in (2, 3):
        for k in range(2):
            ring_fwd(m, 1, k, 0)
    for m in (2, 3, 0, 1):
        for k in range(2):
            arrived(ring, m, 0, k, None, 2)
            second(m, k, 2)
    arrived(tail_ring, 0, 1)
    arrived(tail_ring, 0, 2)
    for j in range(2):
        start(tail_ring, 1, j)
    for k in range(2):
        for m in (2, 3):
            ring_fwd(m, 1, k, -1)
            ring_fwd(m, 1, k, 1)
    arrived(tail_ring, 1, 0)
    start(tail_ring, 1, 2)
    for k in range(2):
        for m in (2, 3):
            ring_fwd(m, 1, k, 2)
            start(cross, m, k, None, -1 if k == 0 else 1)
    for m in (0, 1):
        ring_start(m, 1, 0)
    arrived(tail_ring, 1, 1)
    arrived(tail_ring, 1, 2)
    for k in range(2):
        start(tail_cross, k)

    def second_done(m, k):
        for q in (0, -1, 1, 2):
            ring_fin(m, 1, k, q)
        for i in (1 if k == 0 else -1, 2):
            start(cross, m, k, None, i)

    def crossed(m, k):
        for q in (0, -1, 1, 2):
            arrived(cross, m, k - 2, q, 0)
        if m >= 2:
            for i in (-1, 1, 2):
                arrived(cross, m, k - 2, None, i)
        else:
            ring_start(m, 1, k)

    def e_ready(m):
        e_own(m).wait()
        e_copy(m).wait_recv()

    def stat_copy(n, xx, yy, zz):
        ks = ((0, 2), (2, 1), (3, 1))[n]
        return remote(
            rowed.at[yy * 4 + zz, pl.ds(*ks)], r.at[src, pl.ds(*ks)], r_send.at[n], r_recv.at[n], dev(xx, yy, zz, core)
        )

    def pack(k):
        skew = lax.rem(
            lax.broadcasted_iota(jnp.int32, (8, 128), 1) // 16 - lax.broadcasted_iota(jnp.int32, (8, 128), 0) + 8, 8
        )
        for half in range(2):
            tile = stat[half, k]
            out = tile
            for d in range(1, 8):
                out = jnp.where(skew == d, pltpu.roll(pltpu.roll(tile, 8 - d, 0), 16 * d, 1), out)
            for i in range(8):
                rowed[half * 8 + i, k] = out[i : i + 1, :]

    def send_all(n, xx, first):
        def step(i, carry):
            stat_copy(n, xx, wrap(y + i // 4), wrap(z + lax.rem(i, 4))).start()
            return carry

        lax.fori_loop(first, 16, step, 0)

    def comm(t):
        if t == 0:
            for m in (0, 1):
                ring_start(m, 1, 1)
            for k in range(2):
                for m in (2, 3):
                    second_done(m, k)
            e_ready(2)
        if t == 1:
            e_ready(3)
            for k in range(2):
                arrived(tail_cross, k)
            group = lax.broadcasted_iota(jnp.int32, (8, 128), 1) // 16
            for k in range(4):
                for half in range(2):
                    lanes = jnp.zeros((8, 128), jnp.int32)
                    for i in range(8):
                        lanes = jnp.where(group == i, tb[k, half * 2 + i // 4, i % 4], lanes)
                    tv[k, :, half * 128 : half * 128 + 128] = lanes
        if t == 2:
            ring_fwd(0, 1, 0)
            ring_fwd(1, 1, 0)
        if t == 3:
            ring_fwd(0, 1, 1)
            ring_fwd(1, 1, 1)
        if t == 4:
            e_ready(0)
            crossed(0, 2)
            crossed(1, 2)
            ring_fin(0, 1, 0)
        if t == 5:
            e_ready(1)
            crossed(0, 3)
            crossed(1, 3)
            ring_fin(1, 1, 0)
        if t == 6:
            ring_fin(0, 1, 1)
        if t == 7:
            ring_fin(1, 1, 1)
            ring_fwd(0, 1, 2)
            ring_fwd(1, 1, 2)
        if t == 8:
            crossed(2, 2)
        if t == 9:
            ring_fwd(0, 1, 3)
            ring_fwd(1, 1, 3)
            crossed(2, 3)
        if t == 10:
            pack(0)
            pack(1)
            pltpu.make_async_copy(rowed.at[src, pl.ds(0, 2)], r.at[src, pl.ds(0, 2)], r_recv.at[0]).start()
            send_all(0, x, 1)
            ring_fin(0, 1, 2)
        if t == 11:
            ring_fin(1, 1, 2)
        if t == 12:
            ring_fin(0, 1, 3)
        if t == 13:
            ring_fin(1, 1, 3)
        if t == 14:
            crossed(3, 2)
        if t == 15:
            crossed(3, 3)

    sub = lax.broadcasted_iota(jnp.int32, (8, 256), 0)
    blocks = rows // 8

    def dot(out, m, k):
        right = u[m, k].reshape(256, width)
        for j in range(2):
            out[j * rows : j * rows + rows, :] = lax.dot_general(
                e[j, m], right, (((1,), (1,)), ((), ())), preferred_element_type=F32
            )

    def process(ref, m, k):
        rel = [tv[k] - (idx + j * (1 - 2 * core)) * rows - sub for j in range(2)]
        tops = [ref[8 * i : 8 * i + 8, :] for i in range(4)]
        for i in range(4, 2 * blocks):
            tops[i % 4] = jnp.maximum(tops[i % 4], ref[8 * i : 8 * i + 8, :])
        top = jnp.maximum(jnp.maximum(tops[0], tops[1]), jnp.maximum(tops[2], tops[3]))
        top = jnp.max(top, axis=0, keepdims=True)
        wide = jnp.broadcast_to(top, (8, 256))
        sums = [jnp.zeros((8, 256), F32)] * 4
        true = [jnp.zeros((8, 256), F32)] * 2
        for i in range(2 * blocks):
            v = ref[8 * i : 8 * i + 8, :]
            sums[i % 4] = sums[i % 4] + jnp.exp(v - wide)
            j = i // blocks
            true[j] = jnp.where(rel[j] == 8 * (i % blocks), v, true[j])
        total = jnp.sum((sums[0] + sums[1]) + (sums[2] + sums[3]), axis=0, keepdims=True)
        lse = top + jnp.log(total)
        tail = jnp.sum(true[0] + true[1], axis=0, keepdims=True)
        for half in range(2):
            cols = slice(half * 128, half * 128 + 128)
            stat[half, k, pl.ds(m, 1), :] = lse[:, cols]
            stat[half, k, pl.ds(m + 4, 1), :] = tail[:, cols]

    s1[...] = jnp.zeros_like(s1)
    tv[...] = jnp.zeros_like(tv)

    def batches(i, carry):
        for p in range(2):
            t = 2 * i + p
            for j in range(p, 16, 2):
                pl.when(i == j // 2)(lambda j=j: comm(j))
            old = jnp.maximum(t - 1, 0)
            dot((s0, s1)[p], lookup(BATCH_M, t), lookup(BATCH_K, t))
            process((s1, s0)[p], lookup(BATCH_M, old), lookup(BATCH_K, old))
        return carry

    lax.fori_loop(0, 8, batches, 0)
    pack(2)
    send_all(1, wrap(x - 1), 0)
    process(s1, BATCH_M[15], BATCH_K[15])
    pack(3)
    send_all(2, wrap(x + 1), 0)

    whole = (r.at[:, pl.ds(0, 2)], r.at[:, pl.ds(2, 1)], r.at[:, pl.ds(3, 1)])
    part = r.at[pl.ds(0, 15), pl.ds(0, 2)]
    pltpu.make_async_copy(whole[0], whole[0], r_recv.at[0]).wait()
    pltpu.make_async_copy(part, part, r_send.at[0]).wait()

    def reduce(k):
        tiles = [r[i, k] for i in range(16)]
        top = tiles[0]
        total = tiles[0]
        for tile in tiles[1:]:
            top = jnp.maximum(top, tile)
            total = total + tile
        mass = jnp.exp(tiles[0] - top)
        for tile in tiles[1:]:
            mass = mass + jnp.exp(tile - top)
        return top, mass, total

    near = [reduce(0), reduce(1)]
    for copies in list(sent):
        make, args = copies
        make(*args).wait_send()
    for m in range(4):
        e_copy(m).wait_send()
    def half_turn(v):
        return pltpu.roll(jnp.broadcast_to(v, (8, 128)), 64, 1)[0:1, :]

    values = []
    for h in range(2):
        pltpu.make_async_copy(whole[1 + h], whole[1 + h], r_recv.at[1 + h]).wait()
        top0, mass0, total0 = near[h]
        top1, mass1, total1 = reduce(h + 2)
        top = jnp.maximum(top0, top1)
        lse = top + jnp.log(mass0 * jnp.exp(top0 - top) + mass1 * jnp.exp(top1 - top))
        total = total0 + total1
        values.append(half_turn(total) - lse if h == 0 else total - half_turn(lse))
    row[...] = jnp.where(lax.broadcasted_iota(jnp.int32, (1, 128), 1) < 64, values[0], values[1])

    pltpu.make_async_copy(row, g.at[idx], g_recv.at[0]).start()

    def g_step(i, carry):
        to = {"ent": lax.rem(idx + i, 64), "rep": rep}
        remote(row, g.at[idx], g_send.at[0], g_recv.at[0], to).start()
        return carry

    lax.fori_loop(1, 64, g_step, 0)
    order = order_ref[...]
    sub32 = lax.broadcasted_iota(jnp.int32, order.shape, 0)
    owner = order // 32
    inside = lax.rem(order // 16, 2) * 64 + lax.rem(order, 16)
    lane32 = lax.broadcasted_iota(jnp.int32, order.shape, 1)
    for n in range(2):
        pltpu.make_async_copy(whole[1 + n], whole[1 + n], r_send.at[1 + n]).wait()
    part = g.at[pl.ds(0, 63)]
    pltpu.make_async_copy(part, part, g_send.at[0]).wait()
    pltpu.make_async_copy(g, g, g_recv.at[0]).wait()

    picked = jnp.zeros(order.shape, F32)
    for i in range(64):
        picked = jnp.where(owner == i, g[i], picked)
    cols = []
    for m in range(4):
        col = jnp.sum(jnp.where(lane32 == inside + m * 16, picked, 0.0), axis=1, keepdims=True)
        cols.append(col)
    best = jnp.maximum(jnp.maximum(cols[0], cols[1]), jnp.maximum(cols[2], cols[3]))
    mean = sum(jnp.exp(c - best) for c in cols) * 0.25
    diagonal = sub32 == lane32
    out_ref[...] = jnp.zeros_like(out_ref)
    for m, col in enumerate(cols + [best + jnp.log(mean)]):
        out_ref[m : m + 1, :] = jnp.sum(jnp.where(diagonal, col, 0.0), axis=0, keepdims=True)


def build_kernel(
    head_ref, rel_ref, order_ref, tail_ref, ent_ref, table_ref, q_ref, tails_ref, wide_ref,
    head_rows, rel_rows, qf, sem,
):
    rows, width = ent_ref.shape[1:]
    half_width = width // 2
    offset = lax.axis_index("ent") * rows

    def fetch(i, carry):
        head = pl.multiple_of((head_ref[i] - offset) // 16 * 16, 16)
        pltpu.make_async_copy(ent_ref.at[:, pl.ds(head, 16)], head_rows.at[i], sem.at[0]).start()
        pltpu.make_async_copy(table_ref.at[rel_ref[i]], rel_rows.at[i], sem.at[1]).start()
        return carry

    lax.fori_loop(0, 32, fetch, 0, unroll=4)
    lane16 = lax.rem(lax.broadcasted_iota(jnp.int32, (1, 128), 1), 16)
    for k in range(2):
        acc = jnp.zeros((1, 128), jnp.int32)
        for i in range(16):
            acc = jnp.where(lane16 == i, tail_ref[k * 16 + i], acc)
        tails_ref[k] = acc
    for i in range(32):
        wide_ref[i : i + 1, :] = jnp.full((1, 128), order_ref[i], jnp.int32)
    pltpu.make_async_copy(rel_rows, rel_rows, sem.at[1]).wait()
    pltpu.make_async_copy(head_rows, head_rows, sem.at[0]).wait()
    sub16 = lax.broadcasted_iota(jnp.int32, (16, width), 0)

    def pick(i, carry):
        hit = sub16 == lax.rem(head_ref[i], 16)
        right = rel_rows[i].astype(F32)
        for m in range(4):
            left = jnp.sum(jnp.where(hit, head_rows[i, m].astype(F32), 0.0), axis=0, keepdims=True)
            a, b = left[:, :half_width], left[:, half_width:]
            c, d = right[m : m + 1, :half_width], right[m : m + 1, half_width:]
            qf[m, pl.ds(i, 1), :half_width] = a * c - b * d
            qf[m, pl.ds(i, 1), half_width:] = a * d + b * c
        return carry

    lax.fori_loop(0, 32, pick, 0, unroll=4)
    q_ref[...] = qf[...].astype(BF16)


def per_device(entity_table, relation_table, head_ids, relation_ids, order, tail_ids):
    members, local_count, width = entity_table.shape
    vmem = pl.BlockSpec(memory_space=pltpu.VMEM)
    smem = pl.BlockSpec(memory_space=pltpu.SMEM)
    hbm = pl.BlockSpec(memory_space=pl.ANY)
    dma = pltpu.SemaphoreType.DMA
    query, tails, order_wide = pl.pallas_call(
        build_kernel,
        out_shape=(
            jax.ShapeDtypeStruct((members, 32, width), BF16),
            jax.ShapeDtypeStruct((2, 1, 128), jnp.int32),
            jax.ShapeDtypeStruct((32, 128), jnp.int32),
        ),
        in_specs=[smem, smem, smem, smem, hbm, hbm],
        out_specs=(vmem, vmem, vmem),
        scratch_shapes=[
            pltpu.VMEM((32, members, 16, width), BF16),
            pltpu.VMEM((32, members, width), BF16),
            pltpu.VMEM((members, 32, width), F32),
            dma((2,)),
        ],
        compiler_params=pltpu.CompilerParams(vmem_limit_bytes=58 * 1024 * 1024),
        name="build_queries",
    )(head_ids, relation_ids, order, tail_ids, entity_table, jnp.transpose(relation_table, (1, 0, 2)))
    out = pl.pallas_call(
        score_kernel,
        out_shape=jax.ShapeDtypeStruct((8, 128), F32),
        in_specs=[vmem, vmem, vmem, hbm],
        out_specs=vmem,
        scratch_shapes=[
            pltpu.VMEM((4, 4, 4, 4, 16, width), BF16),
            pltpu.VMEM((2, 4, local_count, width), BF16),
            pltpu.VMEM((2 * local_count, 256), F32),
            pltpu.VMEM((2 * local_count, 256), F32),
            pltpu.VMEM((4, 4, 4, 1, 128), jnp.int32),
            pltpu.VMEM((4, 8, 256), jnp.int32),
            pltpu.VMEM((2, 4, 8, 128), F32),
            pltpu.VMEM((16, 4, 1, 128), F32),
            pltpu.VMEM((16, 4, 1, 128), F32),
            pltpu.VMEM((1, 128), F32),
            pltpu.VMEM((64, 1, 128), F32),
            dma((N_MSG,)),
            dma((N_MSG,)),
            dma((4,)),
            dma((4,)),
            dma((4,)),
            dma((3,)),
            dma((3,)),
            dma((1,)),
            dma((1,)),
        ],
        compiler_params=pltpu.CompilerParams(
            collective_id=0, has_side_effects=True, vmem_limit_bytes=58 * 1024 * 1024
        ),
        cost_estimate=pl.CostEstimate(
            flops=2 * members * 2048 * local_count * width,
            bytes_accessed=4 * members * local_count * width,
            transcendentals=members * 2048 * local_count,
        ),
        name="score_exchange",
    )(query, tails, order_wide, entity_table)
    return (out[4, :32], out[:4, :32].T)


def solution(mesh):
    placed = (
        P(None, "ent", None),
        P(),
        P(("rep", "ent")),
        P(("rep", "ent")),
        P(("rep", "ent")),
        P(("rep", "ent")),
    )
    return jax.shard_map(
        per_device,
        mesh=mesh,
        in_specs=placed,
        out_specs=(P(("rep", "ent")), P(("rep", "ent"), None)),
        check_vma=False,
    )
```

```python
import jax
import jax.numpy as jnp
from jax import lax
from jax.experimental import pallas as pl
from jax.experimental.pallas import tpu as pltpu
from jax.sharding import PartitionSpec as P

MESH = pl.DeviceIdType.MESH
F32 = jnp.float32
BF16 = jnp.bfloat16

AXES = ("yz", "zy", "yz", "zy")
BATCH_M = (2, 3, 2, 3, 0, 1, 0, 1, 2, 2, 0, 1, 3, 3, 0, 1)
BATCH_K = (0, 0, 1, 1, 0, 0, 1, 1, 2, 3, 2, 2, 2, 3, 3, 3)
N_MSG = 160


def lookup(table, t):
    low = sum(v << (2 * i) for i, v in enumerate(table[:8]))
    high = sum(v << (2 * i) for i, v in enumerate(table[8:]))
    return (jnp.where(t < 8, low, high) >> (2 * lax.rem(t, 8))) & 3


def score_kernel(
    q_ref, tails_ref, order_ref, ent_ref, out_ref,
    u, e, s0, s1, tb, tv, stat, rowed, r, row, g,
    send, recv, e_local, e_send, e_recv, r_send, r_recv, g_send, g_recv,
):
    rows, width = e.shape[2:]
    idx = lax.axis_index("ent")
    rep = lax.axis_index("rep")
    core = lax.rem(idx, 2)
    x_lo = lax.rem(idx // 2, 2)
    x = rep * 2 + x_lo
    y = lax.rem(idx // 4, 4)
    z = idx // 16
    src = y * 4 + z

    def dev(xx, yy, zz, cc):
        return {"ent": ((zz * 4 + yy) * 2 + lax.rem(xx, 2)) * 2 + cc, "rep": xx // 2}

    def wrap(v):
        return lax.rem(v + 4, 4)

    def along(axis, shift):
        if axis == "x":
            return dev(wrap(x + shift), y, z, core)
        return dev(x, wrap(y + shift), z, core) if axis == "y" else dev(x, y, wrap(z + shift), core)

    def remote(a, b, send_sem, recv_sem, to):
        return pltpu.make_async_remote_copy(
            src_ref=a, dst_ref=b, send_sem=send_sem, recv_sem=recv_sem, device_id=to, device_id_type=MESH
        )

    def e_own(m):
        return pltpu.make_async_copy(ent_ref.at[m], e.at[0, m], e_local.at[m])

    def e_copy(m):
        return remote(ent_ref.at[m], e.at[1, m], e_send.at[m], e_recv.at[m], dev(x, y, z, 1 - core))

    for m in (2, 3, 0, 1):
        e_own(m).start()

    barrier = pltpu.get_barrier_semaphore()
    partners = [along(axis, shift) for axis in "xyz" for shift in (1, -1)] + [dev(x, y, z, 1 - core)]
    for partner in partners:
        pl.semaphore_signal(barrier, inc=1, device_id=partner, device_id_type=MESH)

    for m in range(4):
        for k in range(2):
            u[m, k, y, z] = q_ref[m, 16 * k : 16 * k + 16, :]
    for k in range(2):
        tb[k, y, z] = tails_ref[k]
    pl.semaphore_wait(barrier, len(partners))

    numbers = {}
    sent = {}

    def sem_of(key):
        return numbers.setdefault(key, len(numbers))

    def at(m, k, first, second):
        return u.at[m, k, first, second] if AXES[m][0] == "y" else u.at[m, k, second, first]

    def own(m, ph):
        return y if AXES[m][ph] == "y" else z

    def piece(m, q):
        return slice(None) if q is None else wrap(own(m, 0) + q)

    def ring(m, ph, k, q, j):
        offset, shift = ((0, 1), (0, -1), (-1, 1) if k % 2 == 0 else (1, -1))[j]
        pos = wrap(own(m, ph) + offset)
        ref = at(m, k, pos, own(m, 1)) if ph == 0 else at(m, k, piece(m, q), pos)
        n = sem_of((m, ph, k, q, j))
        return remote(ref, ref, send.at[n], recv.at[n], along(AXES[m][ph], shift))

    def cross(m, k, q, i):
        pos = wrap(own(m, 1) + i)
        n = sem_of((m, k, q, i))
        return remote(
            at(m, k, piece(m, q), pos), at(m, k + 2, piece(m, q), pos), send.at[n], recv.at[n],
            along("x", 1 if k == 0 else -1),
        )

    def tail_ring(ph, j):
        offset, shift = ((0, 1), (0, -1), (-1, 1))[j]
        ref = tb.at[pl.ds(0, 2), wrap(y + offset), z] if ph == 0 else tb.at[pl.ds(0, 2), :, wrap(z + offset)]
        n = sem_of(("tail", ph, j))
        return remote(ref, ref, send.at[n], recv.at[n], along("yz"[ph], shift))

    def tail_cross(k):
        n = sem_of(("tail", k))
        return remote(tb.at[k], tb.at[k + 2], send.at[n], recv.at[n], along("x", 1 if k == 0 else -1))

    def start(make, *args):
        make(*args).start()
        sent[(make, args)] = True

    def arrived(make, *args):
        make(*args).wait_recv()

    def ring_start(m, ph, k, q=None):
        start(ring, m, ph, k, q, 0)
        start(ring, m, ph, k, q, 1)

    def ring_fwd(m, ph, k, q=None):
        arrived(ring, m, ph, k, q, k % 2)
        start(ring, m, ph, k, q, 2)

    def ring_fin(m, ph, k, q=None):
        arrived(ring, m, ph, k, q, 1 - k % 2)
        arrived(ring, m, ph, k, q, 2)

    for m in (2, 3, 0, 1):
        if m == 0:
            for j in range(2):
                start(tail_ring, 0, j)
        for k in range(2):
            ring_start(m, 0, k)
        for k in range(2):
            if m >= 2:
                ring_start(m, 1, k, 0)
            start(cross, m, k, 0, 0)
    for m in (2, 3, 0, 1):
        e_copy(m).start()

    def second(m, k, q):
        if m >= 2:
            ring_start(m, 1, k, q)
        start(cross, m, k, q, 0)

    for m in (2, 3, 0, 1):
        for k in range(2):
            ring_fwd(m, 0, k)
            second(m, k, -1 if k == 0 else 1)
        for k in range(2):
            arrived(ring, m, 0, k, None, 1 - k)
            second(m, k, 1 if k == 0 else -1)
    arrived(tail_ring, 0, 0)
    start(tail_ring, 0, 2)
    for m in (2, 3):
        for k in range(2):
            ring_fwd(m, 1, k, 0)
    for m in (2, 3, 0, 1):
        for k in range(2):
            arrived(ring, m, 0, k, None, 2)
            second(m, k, 2)
    arrived(tail_ring, 0, 1)
    arrived(tail_ring, 0, 2)
    for j in range(2):
        start(tail_ring, 1, j)
    for k in range(2):
        for m in (2, 3):
            ring_fwd(m, 1, k, -1)
            ring_fwd(m, 1, k, 1)
    arrived(tail_ring, 1, 0)
    start(tail_ring, 1, 2)
    for k in range(2):
        for m in (2, 3):
            ring_fwd(m, 1, k, 2)
            start(cross, m, k, None, -1 if k == 0 else 1)
    for m in (0, 1):
        ring_start(m, 1, 0)
    arrived(tail_ring, 1, 1)
    arrived(tail_ring, 1, 2)
    for k in range(2):
        start(tail_cross, k)

    def second_done(m, k):
        for q in (0, -1, 1, 2):
            ring_fin(m, 1, k, q)
        for i in (1 if k == 0 else -1, 2):
            start(cross, m, k, None, i)

    def crossed(m, k):
        for q in (0, -1, 1, 2):
            arrived(cross, m, k - 2, q, 0)
        if m >= 2:
            for i in (-1, 1, 2):
                arrived(cross, m, k - 2, None, i)
        else:
            ring_start(m, 1, k)

    def e_ready(m):
        e_own(m).wait()
        e_copy(m).wait_recv()

    def stat_copy(n, xx, yy, zz):
        ks = ((0, 2), (2, 1), (3, 1))[n]
        return remote(
            rowed.at[yy * 4 + zz, pl.ds(*ks)], r.at[src, pl.ds(*ks)], r_send.at[n], r_recv.at[n], dev(xx, yy, zz, core)
        )

    def pack(k):
        skew = lax.rem(
            lax.broadcasted_iota(jnp.int32, (8, 128), 1) // 16 - lax.broadcasted_iota(jnp.int32, (8, 128), 0) + 8, 8
        )
        for half in range(2):
            tile = stat[half, k]
            out = tile
            for d in range(1, 8):
                out = jnp.where(skew == d, pltpu.roll(pltpu.roll(tile, 8 - d, 0), 16 * d, 1), out)
            for i in range(8):
                rowed[half * 8 + i, k] = out[i : i + 1, :]

    def send_all(n, xx, first):
        def step(i, carry):
            stat_copy(n, xx, wrap(y + i // 4), wrap(z + lax.rem(i, 4))).start()
            return carry

        lax.fori_loop(first, 16, step, 0)

    def comm(t):
        if t == 0:
            crossed(0, 2)
            crossed(1, 2)
            for m in (0, 1):
                ring_start(m, 1, 1)
            for k in range(2):
                for m in (2, 3):
                    second_done(m, k)
            e_ready(2)
        if t == 1:
            crossed(0, 3)
            crossed(1, 3)
            ring_fwd(0, 1, 0)
            ring_fwd(1, 1, 0)
            e_ready(3)
            for k in range(2):
                arrived(tail_cross, k)
            group = lax.broadcasted_iota(jnp.int32, (8, 128), 1) // 16
            for k in range(4):
                for half in range(2):
                    lanes = jnp.zeros((8, 128), jnp.int32)
                    for i in range(8):
                        lanes = jnp.where(group == i, tb[k, half * 2 + i // 4, i % 4], lanes)
                    tv[k, :, half * 128 : half * 128 + 128] = lanes
        if t == 2:
            ring_fwd(0, 1, 1)
            ring_fwd(1, 1, 1)
        if t == 4:
            e_ready(0)
            ring_fin(0, 1, 0)
        if t == 5:
            ring_fwd(0, 1, 2)
            ring_fwd(1, 1, 2)
            e_ready(1)
            ring_fin(1, 1, 0)
        if t == 6:
            ring_fin(0, 1, 1)
        if t == 7:
            ring_fin(1, 1, 1)
        if t == 8:
            ring_fwd(0, 1, 3)
            ring_fwd(1, 1, 3)
            crossed(2, 2)
        if t == 9:
            crossed(2, 3)
        if t == 10:
            pack(0)
            pack(1)
            pltpu.make_async_copy(rowed.at[src, pl.ds(0, 2)], r.at[src, pl.ds(0, 2)], r_recv.at[0]).start()
            send_all(0, x, 1)
            ring_fin(0, 1, 2)
        if t == 11:
            ring_fin(1, 1, 2)
        if t == 12:
            crossed(3, 2)
        if t == 13:
            crossed(3, 3)
        if t == 14:
            ring_fin(0, 1, 3)
        if t == 15:
            ring_fin(1, 1, 3)

    sub = lax.broadcasted_iota(jnp.int32, (8, 256), 0)
    blocks = rows // 8

    def dot(out, m, k):
        right = u[m, k].reshape(256, width)
        for j in range(2):
            out[j * rows : j * rows + rows, :] = lax.dot_general(
                e[j, m], right, (((1,), (1,)), ((), ())), preferred_element_type=F32
            )

    def process(ref, m, k):
        rel = [tv[k] - (idx + j * (1 - 2 * core)) * rows - sub for j in range(2)]
        tops = [ref[8 * i : 8 * i + 8, :] for i in range(4)]
        for i in range(4, 2 * blocks):
            tops[i % 4] = jnp.maximum(tops[i % 4], ref[8 * i : 8 * i + 8, :])
        top = jnp.maximum(jnp.maximum(tops[0], tops[1]), jnp.maximum(tops[2], tops[3]))
        top = jnp.max(top, axis=0, keepdims=True)
        wide = jnp.broadcast_to(top, (8, 256))
        sums = [jnp.zeros((8, 256), F32)] * 4
        true = [jnp.zeros((8, 256), F32)] * 2
        for i in range(2 * blocks):
            v = ref[8 * i : 8 * i + 8, :]
            sums[i % 4] = sums[i % 4] + jnp.exp(v - wide)
            j = i // blocks
            true[j] = jnp.where(rel[j] == 8 * (i % blocks), v, true[j])
        total = jnp.sum((sums[0] + sums[1]) + (sums[2] + sums[3]), axis=0, keepdims=True)
        lse = top + jnp.log(total)
        tail = jnp.sum(true[0] + true[1], axis=0, keepdims=True)
        for half in range(2):
            cols = slice(half * 128, half * 128 + 128)
            stat[half, k, pl.ds(m, 1), :] = lse[:, cols]
            stat[half, k, pl.ds(m + 4, 1), :] = tail[:, cols]

    s1[...] = jnp.zeros_like(s1)
    tv[...] = jnp.zeros_like(tv)

    def batches(i, carry):
        for p in range(2):
            t = 2 * i + p
            for j in range(p, 16, 2):
                pl.when(i == j // 2)(lambda j=j: comm(j))
            old = jnp.maximum(t - 1, 0)
            dot((s0, s1)[p], lookup(BATCH_M, t), lookup(BATCH_K, t))
            process((s1, s0)[p], lookup(BATCH_M, old), lookup(BATCH_K, old))
        return carry

    lax.fori_loop(0, 8, batches, 0)
    pack(2)
    send_all(1, wrap(x - 1), 0)
    process(s1, BATCH_M[15], BATCH_K[15])
    pack(3)
    send_all(2, wrap(x + 1), 0)

    whole = (r.at[:, pl.ds(0, 2)], r.at[:, pl.ds(2, 1)], r.at[:, pl.ds(3, 1)])
    part = r.at[pl.ds(0, 15), pl.ds(0, 2)]
    pltpu.make_async_copy(whole[0], whole[0], r_recv.at[0]).wait()
    pltpu.make_async_copy(part, part, r_send.at[0]).wait()

    def reduce(k):
        tiles = [r[i, k] for i in range(16)]
        top = tiles[0]
        total = tiles[0]
        for tile in tiles[1:]:
            top = jnp.maximum(top, tile)
            total = total + tile
        mass = jnp.exp(tiles[0] - top)
        for tile in tiles[1:]:
            mass = mass + jnp.exp(tile - top)
        return top, mass, total

    near = [reduce(0), reduce(1)]
    for copies in list(sent):
        make, args = copies
        make(*args).wait_send()
    for m in range(4):
        e_copy(m).wait_send()
    def half_turn(v):
        return pltpu.roll(jnp.broadcast_to(v, (8, 128)), 64, 1)[0:1, :]

    values = []
    for h in range(2):
        pltpu.make_async_copy(whole[1 + h], whole[1 + h], r_recv.at[1 + h]).wait()
        top0, mass0, total0 = near[h]
        top1, mass1, total1 = reduce(h + 2)
        top = jnp.maximum(top0, top1)
        lse = top + jnp.log(mass0 * jnp.exp(top0 - top) + mass1 * jnp.exp(top1 - top))
        total = total0 + total1
        values.append(half_turn(total) - lse if h == 0 else total - half_turn(lse))
    row[...] = jnp.where(lax.broadcasted_iota(jnp.int32, (1, 128), 1) < 64, values[0], values[1])

    pltpu.make_async_copy(row, g.at[idx], g_recv.at[0]).start()

    def g_step(i, carry):
        to = {"ent": lax.rem(idx + i, 64), "rep": rep}
        remote(row, g.at[idx], g_send.at[0], g_recv.at[0], to).start()
        return carry

    lax.fori_loop(1, 64, g_step, 0)
    order = order_ref[...]
    sub32 = lax.broadcasted_iota(jnp.int32, order.shape, 0)
    owner = order // 32
    inside = lax.rem(order // 16, 2) * 64 + lax.rem(order, 16)
    lane32 = lax.broadcasted_iota(jnp.int32, order.shape, 1)
    for n in range(2):
        pltpu.make_async_copy(whole[1 + n], whole[1 + n], r_send.at[1 + n]).wait()
    part = g.at[pl.ds(0, 63)]
    pltpu.make_async_copy(part, part, g_send.at[0]).wait()
    pltpu.make_async_copy(g, g, g_recv.at[0]).wait()

    picked = jnp.zeros(order.shape, F32)
    for i in range(64):
        picked = jnp.where(owner == i, g[i], picked)
    cols = []
    for m in range(4):
        col = jnp.sum(jnp.where(lane32 == inside + m * 16, picked, 0.0), axis=1, keepdims=True)
        cols.append(col)
    best = jnp.maximum(jnp.maximum(cols[0], cols[1]), jnp.maximum(cols[2], cols[3]))
    mean = sum(jnp.exp(c - best) for c in cols) * 0.25
    diagonal = sub32 == lane32
    out_ref[...] = jnp.zeros_like(out_ref)
    for m, col in enumerate(cols + [best + jnp.log(mean)]):
        out_ref[m : m + 1, :] = jnp.sum(jnp.where(diagonal, col, 0.0), axis=0, keepdims=True)


def build_kernel(
    head_ref, rel_ref, order_ref, tail_ref, ent_ref, table_ref, q_ref, tails_ref, wide_ref,
    head_rows, rel_rows, relf, head_at, sem,
):
    rows, width = ent_ref.shape[1:]
    half_width = width // 2
    offset = lax.axis_index("ent") * rows

    def fetch(i, carry):
        head = pl.multiple_of((head_ref[i] - offset) // 16 * 16, 16)
        pltpu.make_async_copy(ent_ref.at[:, pl.ds(head, 16)], head_rows.at[i], sem.at[0]).start()
        pltpu.make_async_copy(table_ref.at[rel_ref[i]], rel_rows.at[i], sem.at[1]).start()
        return carry

    lax.fori_loop(0, 32, fetch, 0, unroll=4)
    lane16 = lax.rem(lax.broadcasted_iota(jnp.int32, (1, 128), 1), 16)
    for k in range(2):
        acc = jnp.zeros((1, 128), jnp.int32)
        for i in range(16):
            acc = jnp.where(lane16 == i, tail_ref[k * 16 + i], acc)
        tails_ref[k] = acc
    for i in range(32):
        wide_ref[i : i + 1, :] = jnp.full((1, 128), order_ref[i], jnp.int32)
        head_at[i : i + 1, :] = jnp.full((1, 128), lax.rem(head_ref[i], 16), jnp.int32)
    pltpu.make_async_copy(rel_rows, rel_rows, sem.at[1]).wait()
    def spread(i, carry):
        right = rel_rows[i].astype(F32)
        for m in range(4):
            relf[m, pl.ds(i, 1), :] = right[m : m + 1, :]
        return carry

    lax.fori_loop(0, 32, spread, 0, unroll=8)
    pltpu.make_async_copy(head_rows, head_rows, sem.at[0]).wait()
    lane = lax.broadcasted_iota(jnp.int32, (32, 128), 1)
    sub = lax.broadcasted_iota(jnp.int32, (32, 128), 0)
    inside = lax.rem(lane, 16) == head_at[...]
    picker = jnp.concatenate(
        [jnp.where(jnp.logical_and(inside, lane // 16 + 8 * c == sub), 1.0, 0.0) for c in range(4)], axis=1
    ).astype(BF16)
    for m in range(4):
        left = jnp.dot(picker, head_rows[:, m].reshape(512, width), preferred_element_type=F32)
        a, b = left[:, :half_width], left[:, half_width:]
        c, d = relf[m, :, :half_width], relf[m, :, half_width:]
        q_ref[m, :, :half_width] = (a * c - b * d).astype(BF16)
        q_ref[m, :, half_width:] = (a * d + b * c).astype(BF16)


def per_device(entity_table, relation_table, head_ids, relation_ids, order, tail_ids):
    members, local_count, width = entity_table.shape
    vmem = pl.BlockSpec(memory_space=pltpu.VMEM)
    smem = pl.BlockSpec(memory_space=pltpu.SMEM)
    hbm = pl.BlockSpec(memory_space=pl.ANY)
    dma = pltpu.SemaphoreType.DMA
    query, tails, order_wide = pl.pallas_call(
        build_kernel,
        out_shape=(
            jax.ShapeDtypeStruct((members, 32, width), BF16),
            jax.ShapeDtypeStruct((2, 1, 128), jnp.int32),
            jax.ShapeDtypeStruct((32, 128), jnp.int32),
        ),
        in_specs=[smem, smem, smem, smem, hbm, hbm],
        out_specs=(vmem, vmem, vmem),
        scratch_shapes=[
            pltpu.VMEM((32, members, 16, width), BF16),
            pltpu.VMEM((32, members, width), BF16),
            pltpu.VMEM((members, 32, width), F32),
            pltpu.VMEM((32, 128), jnp.int32),
            dma((2,)),
        ],
        compiler_params=pltpu.CompilerParams(vmem_limit_bytes=58 * 1024 * 1024),
        name="build_queries",
    )(head_ids, relation_ids, order, tail_ids, entity_table, jnp.transpose(relation_table, (1, 0, 2)))
    out = pl.pallas_call(
        score_kernel,
        out_shape=jax.ShapeDtypeStruct((8, 128), F32),
        in_specs=[vmem, vmem, vmem, hbm],
        out_specs=vmem,
        scratch_shapes=[
            pltpu.VMEM((4, 4, 4, 4, 16, width), BF16),
            pltpu.VMEM((2, 4, local_count, width), BF16),
            pltpu.VMEM((2 * local_count, 256), F32),
            pltpu.VMEM((2 * local_count, 256), F32),
            pltpu.VMEM((4, 4, 4, 1, 128), jnp.int32),
            pltpu.VMEM((4, 8, 256), jnp.int32),
            pltpu.VMEM((2, 4, 8, 128), F32),
            pltpu.VMEM((16, 4, 1, 128), F32),
            pltpu.VMEM((16, 4, 1, 128), F32),
            pltpu.VMEM((1, 128), F32),
            pltpu.VMEM((64, 1, 128), F32),
            dma((N_MSG,)),
            dma((N_MSG,)),
            dma((4,)),
            dma((4,)),
            dma((4,)),
            dma((3,)),
            dma((3,)),
            dma((1,)),
            dma((1,)),
        ],
        compiler_params=pltpu.CompilerParams(
            collective_id=0, has_side_effects=True, vmem_limit_bytes=58 * 1024 * 1024
        ),
        cost_estimate=pl.CostEstimate(
            flops=2 * members * 2048 * local_count * width,
            bytes_accessed=4 * members * local_count * width,
            transcendentals=members * 2048 * local_count,
        ),
        name="score_exchange",
    )(query, tails, order_wide, entity_table)
    return (out[4, :32], out[:4, :32].T)


def solution(mesh):
    placed = (
        P(None, "ent", None),
        P(),
        P(("rep", "ent")),
        P(("rep", "ent")),
        P(("rep", "ent")),
        P(("rep", "ent")),
    )
    return jax.shard_map(
        per_device,
        mesh=mesh,
        in_specs=placed,
        out_specs=(P(("rep", "ent")), P(("rep", "ent"), None)),
        check_vma=False,
    )
```

```python
import jax
import jax.numpy as jnp
from jax import lax
from jax.experimental import pallas as pl
from jax.experimental.pallas import tpu as pltpu
from jax.sharding import PartitionSpec as P

MESH = pl.DeviceIdType.MESH
F32 = jnp.float32
BF16 = jnp.bfloat16

AXES = ("yz", "zy", "yz", "zy")
BATCH_M = (2, 3, 2, 3, 0, 1, 0, 1, 2, 2, 0, 1, 3, 3, 0, 1)
BATCH_K = (0, 0, 1, 1, 0, 0, 1, 1, 2, 3, 2, 2, 2, 3, 3, 3)
N_MSG = 160


def lookup(table, t):
    low = sum(v << (2 * i) for i, v in enumerate(table[:8]))
    high = sum(v << (2 * i) for i, v in enumerate(table[8:]))
    return (jnp.where(t < 8, low, high) >> (2 * lax.rem(t, 8))) & 3


def score_kernel(
    q_ref, tails_ref, order_ref, ent_ref, out_ref,
    u, e, s0, s1, tb, tv, stat, rowed, r, row, g,
    send, recv, e_local, e_send, e_recv, r_send, r_recv, g_send, g_recv,
):
    rows, width = e.shape[2:]
    idx = lax.axis_index("ent")
    rep = lax.axis_index("rep")
    core = lax.rem(idx, 2)
    x_lo = lax.rem(idx // 2, 2)
    x = rep * 2 + x_lo
    y = lax.rem(idx // 4, 4)
    z = idx // 16
    src = y * 4 + z

    def dev(xx, yy, zz, cc):
        return {"ent": ((zz * 4 + yy) * 2 + lax.rem(xx, 2)) * 2 + cc, "rep": xx // 2}

    def wrap(v):
        return lax.rem(v + 4, 4)

    def along(axis, shift):
        if axis == "x":
            return dev(wrap(x + shift), y, z, core)
        return dev(x, wrap(y + shift), z, core) if axis == "y" else dev(x, y, wrap(z + shift), core)

    def remote(a, b, send_sem, recv_sem, to):
        return pltpu.make_async_remote_copy(
            src_ref=a, dst_ref=b, send_sem=send_sem, recv_sem=recv_sem, device_id=to, device_id_type=MESH
        )

    def e_own(m):
        return pltpu.make_async_copy(ent_ref.at[m], e.at[0, m], e_local.at[m])

    def e_copy(m):
        return remote(ent_ref.at[m], e.at[1, m], e_send.at[m], e_recv.at[m], dev(x, y, z, 1 - core))

    for m in (2, 3, 0, 1):
        e_own(m).start()

    barrier = pltpu.get_barrier_semaphore()
    partners = [along(axis, shift) for axis in "xyz" for shift in (1, -1)] + [dev(x, y, z, 1 - core)]
    for partner in partners:
        pl.semaphore_signal(barrier, inc=1, device_id=partner, device_id_type=MESH)

    for m in range(4):
        for k in range(2):
            u[m, k, y, z] = q_ref[m, 16 * k : 16 * k + 16, :]
    for k in range(2):
        tb[k, y, z] = tails_ref[k]
    pl.semaphore_wait(barrier, len(partners))

    numbers = {}
    sent = {}

    def sem_of(key):
        return numbers.setdefault(key, len(numbers))

    def at(m, k, first, second):
        return u.at[m, k, first, second] if AXES[m][0] == "y" else u.at[m, k, second, first]

    def own(m, ph):
        return y if AXES[m][ph] == "y" else z

    def piece(m, q):
        return slice(None) if q is None else wrap(own(m, 0) + q)

    def ring(m, ph, k, q, j):
        offset, shift = ((0, 1), (0, -1), (-1, 1) if k % 2 == 0 else (1, -1))[j]
        pos = wrap(own(m, ph) + offset)
        ref = at(m, k, pos, own(m, 1)) if ph == 0 else at(m, k, piece(m, q), pos)
        n = sem_of((m, ph, k, q, j))
        return remote(ref, ref, send.at[n], recv.at[n], along(AXES[m][ph], shift))

    def cross(m, k, q, i):
        pos = wrap(own(m, 1) + i)
        n = sem_of((m, k, q, i))
        return remote(
            at(m, k, piece(m, q), pos), at(m, k + 2, piece(m, q), pos), send.at[n], recv.at[n],
            along("x", 1 if k == 0 else -1),
        )

    def tail_ring(ph, j):
        offset, shift = ((0, 1), (0, -1), (-1, 1))[j]
        ref = tb.at[pl.ds(0, 2), wrap(y + offset), z] if ph == 0 else tb.at[pl.ds(0, 2), :, wrap(z + offset)]
        n = sem_of(("tail", ph, j))
        return remote(ref, ref, send.at[n], recv.at[n], along("yz"[ph], shift))

    def tail_cross(k):
        n = sem_of(("tail", k))
        return remote(tb.at[k], tb.at[k + 2], send.at[n], recv.at[n], along("x", 1 if k == 0 else -1))

    def start(make, *args):
        make(*args).start()
        sent[(make, args)] = True

    def arrived(make, *args):
        make(*args).wait_recv()

    def ring_start(m, ph, k, q=None):
        start(ring, m, ph, k, q, 0)
        start(ring, m, ph, k, q, 1)

    def ring_fwd(m, ph, k, q=None):
        arrived(ring, m, ph, k, q, k % 2)
        start(ring, m, ph, k, q, 2)

    def ring_fin(m, ph, k, q=None):
        arrived(ring, m, ph, k, q, 1 - k % 2)
        arrived(ring, m, ph, k, q, 2)

    for m in (2, 3, 0, 1):
        if m == 0:
            for j in range(2):
                start(tail_ring, 0, j)
        for k in range(2):
            ring_start(m, 0, k)
        for k in range(2):
            if m >= 2:
                ring_start(m, 1, k, 0)
            start(cross, m, k, 0, 0)
    for m in (2, 3, 0, 1):
        e_copy(m).start()

    def second(m, k, q):
        if m >= 2:
            ring_start(m, 1, k, q)
        start(cross, m, k, q, 0)

    for m in (2, 3, 0, 1):
        for k in range(2):
            ring_fwd(m, 0, k)
            second(m, k, -1 if k == 0 else 1)
        for k in range(2):
            arrived(ring, m, 0, k, None, 1 - k)
            second(m, k, 1 if k == 0 else -1)
    arrived(tail_ring, 0, 0)
    start(tail_ring, 0, 2)
    for m in (2, 3):
        for k in range(2):
            ring_fwd(m, 1, k, 0)
    for m in (2, 3, 0, 1):
        for k in range(2):
            arrived(ring, m, 0, k, None, 2)
            second(m, k, 2)
    arrived(tail_ring, 0, 1)
    arrived(tail_ring, 0, 2)
    for j in range(2):
        start(tail_ring, 1, j)
    for k in range(2):
        for m in (2, 3):
            ring_fwd(m, 1, k, -1)
            ring_fwd(m, 1, k, 1)
    arrived(tail_ring, 1, 0)
    start(tail_ring, 1, 2)
    for k in range(2):
        for m in (2, 3):
            ring_fwd(m, 1, k, 2)
            start(cross, m, k, None, -1 if k == 0 else 1)
    for m in (0, 1):
        ring_start(m, 1, 0)
    arrived(tail_ring, 1, 1)
    arrived(tail_ring, 1, 2)
    for k in range(2):
        start(tail_cross, k)

    def second_done(m, k):
        for q in (0, -1, 1, 2):
            ring_fin(m, 1, k, q)
        for i in (1 if k == 0 else -1, 2):
            start(cross, m, k, None, i)

    def crossed(m, k):
        for q in (0, -1, 1, 2):
            arrived(cross, m, k - 2, q, 0)
        if m >= 2:
            for i in (-1, 1, 2):
                arrived(cross, m, k - 2, None, i)
        else:
            ring_start(m, 1, k)

    def e_ready(m):
        e_own(m).wait()
        e_copy(m).wait_recv()

    def stat_copy(n, xx, yy, zz):
        ks = ((0, 2), (2, 1), (3, 1))[n]
        return remote(
            rowed.at[yy * 4 + zz, pl.ds(*ks)], r.at[src, pl.ds(*ks)], r_send.at[n], r_recv.at[n], dev(xx, yy, zz, core)
        )

    def pack(k):
        skew = lax.rem(
            lax.broadcasted_iota(jnp.int32, (8, 128), 1) // 16 - lax.broadcasted_iota(jnp.int32, (8, 128), 0) + 8, 8
        )
        for half in range(2):
            tile = stat[half, k]
            out = tile
            for d in range(1, 8):
                out = jnp.where(skew == d, pltpu.roll(pltpu.roll(tile, 8 - d, 0), 16 * d, 1), out)
            for i in range(8):
                rowed[half * 8 + i, k] = out[i : i + 1, :]

    def far_first(i):
        order = 2 + (1 << 2) + (3 << 4)
        return wrap(y + ((order >> (2 * (i // 4))) & 3)), wrap(z + ((order >> (2 * lax.rem(i, 4))) & 3))

    def send_all(n, xx, count):
        def step(i, carry):
            stat_copy(n, xx, *far_first(i)).start()
            return carry

        lax.fori_loop(0, count, step, 0)

    def comm(t):
        if t == 0:
            crossed(0, 2)
            crossed(1, 2)
            for m in (0, 1):
                ring_start(m, 1, 1)
            for k in range(2):
                for m in (2, 3):
                    second_done(m, k)
            e_ready(2)
        if t == 1:
            crossed(0, 3)
            crossed(1, 3)
            ring_fwd(0, 1, 0)
            ring_fwd(1, 1, 0)
            e_ready(3)
            for k in range(2):
                arrived(tail_cross, k)
            group = lax.broadcasted_iota(jnp.int32, (8, 128), 1) // 16
            for k in range(4):
                for half in range(2):
                    lanes = jnp.zeros((8, 128), jnp.int32)
                    for i in range(8):
                        lanes = jnp.where(group == i, tb[k, half * 2 + i // 4, i % 4], lanes)
                    tv[k, :, half * 128 : half * 128 + 128] = lanes
        if t == 2:
            ring_fwd(0, 1, 1)
            ring_fwd(1, 1, 1)
        if t == 4:
            e_ready(0)
            ring_fin(0, 1, 0)
        if t == 5:
            e_ready(1)
            ring_fin(1, 1, 0)
        if t == 6:
            ring_fwd(0, 1, 2)
            ring_fwd(1, 1, 2)
            ring_fin(0, 1, 1)
        if t == 7:
            ring_fin(1, 1, 1)
        if t == 8:
            crossed(2, 2)
        if t == 9:
            ring_fwd(0, 1, 3)
            ring_fwd(1, 1, 3)
            crossed(2, 3)
        if t == 10:
            pack(0)
            pack(1)
            pltpu.make_async_copy(rowed.at[src, pl.ds(0, 2)], r.at[src, pl.ds(0, 2)], r_recv.at[0]).start()
            send_all(0, x, 15)
            ring_fin(0, 1, 2)
        if t == 11:
            ring_fin(1, 1, 2)
        if t == 12:
            crossed(3, 2)
        if t == 13:
            crossed(3, 3)
        if t == 14:
            ring_fin(0, 1, 3)
        if t == 15:
            ring_fin(1, 1, 3)

    sub = lax.broadcasted_iota(jnp.int32, (8, 256), 0)
    blocks = rows // 8

    def dot(out, m, k):
        right = u[m, k].reshape(256, width)
        for j in range(2):
            out[j * rows : j * rows + rows, :] = lax.dot_general(
                e[j, m], right, (((1,), (1,)), ((), ())), preferred_element_type=F32
            )

    def process(ref, m, k):
        rel = [tv[k] - (idx + j * (1 - 2 * core)) * rows - sub for j in range(2)]
        tops = [ref[8 * i : 8 * i + 8, :] for i in range(4)]
        for i in range(4, 2 * blocks):
            tops[i % 4] = jnp.maximum(tops[i % 4], ref[8 * i : 8 * i + 8, :])
        top = jnp.maximum(jnp.maximum(tops[0], tops[1]), jnp.maximum(tops[2], tops[3]))
        top = jnp.max(top, axis=0, keepdims=True)
        wide = jnp.broadcast_to(top, (8, 256))
        sums = [jnp.zeros((8, 256), F32)] * 4
        true = [jnp.zeros((8, 256), F32)] * 2
        for i in range(2 * blocks):
            v = ref[8 * i : 8 * i + 8, :]
            sums[i % 4] = sums[i % 4] + jnp.exp(v - wide)
            j = i // blocks
            true[j] = jnp.where(rel[j] == 8 * (i % blocks), v, true[j])
        total = jnp.sum((sums[0] + sums[1]) + (sums[2] + sums[3]), axis=0, keepdims=True)
        lse = top + jnp.log(total)
        tail = jnp.sum(true[0] + true[1], axis=0, keepdims=True)
        for half in range(2):
            cols = slice(half * 128, half * 128 + 128)
            stat[half, k, pl.ds(m, 1), :] = lse[:, cols]
            stat[half, k, pl.ds(m + 4, 1), :] = tail[:, cols]

    s1[...] = jnp.zeros_like(s1)
    tv[...] = jnp.zeros_like(tv)

    def batches(i, carry):
        for p in range(2):
            t = 2 * i + p
            for j in range(p, 16, 2):
                pl.when(i == j // 2)(lambda j=j: comm(j))
            old = jnp.maximum(t - 1, 0)
            dot((s0, s1)[p], lookup(BATCH_M, t), lookup(BATCH_K, t))
            process((s1, s0)[p], lookup(BATCH_M, old), lookup(BATCH_K, old))
        return carry

    lax.fori_loop(0, 8, batches, 0)
    pack(2)
    send_all(1, wrap(x - 1), 16)
    process(s1, BATCH_M[15], BATCH_K[15])
    pack(3)
    send_all(2, wrap(x + 1), 16)

    whole = (r.at[:, pl.ds(0, 2)], r.at[:, pl.ds(2, 1)], r.at[:, pl.ds(3, 1)])
    part = r.at[pl.ds(0, 15), pl.ds(0, 2)]
    pltpu.make_async_copy(whole[0], whole[0], r_recv.at[0]).wait()
    pltpu.make_async_copy(part, part, r_send.at[0]).wait()

    def reduce(k):
        tiles = [r[i, k] for i in range(16)]
        top = tiles[0]
        total = tiles[0]
        for tile in tiles[1:]:
            top = jnp.maximum(top, tile)
            total = total + tile
        mass = jnp.exp(tiles[0] - top)
        for tile in tiles[1:]:
            mass = mass + jnp.exp(tile - top)
        return top, mass, total

    near = [reduce(0), reduce(1)]
    for copies in list(sent):
        make, args = copies
        make(*args).wait_send()
    for m in range(4):
        e_copy(m).wait_send()
    def half_turn(v):
        return pltpu.roll(jnp.broadcast_to(v, (8, 128)), 64, 1)[0:1, :]

    values = []
    for h in range(2):
        pltpu.make_async_copy(whole[1 + h], whole[1 + h], r_recv.at[1 + h]).wait()
        top0, mass0, total0 = near[h]
        top1, mass1, total1 = reduce(h + 2)
        top = jnp.maximum(top0, top1)
        lse = top + jnp.log(mass0 * jnp.exp(top0 - top) + mass1 * jnp.exp(top1 - top))
        total = total0 + total1
        values.append(half_turn(total) - lse if h == 0 else total - half_turn(lse))
    row[...] = jnp.where(lax.broadcasted_iota(jnp.int32, (1, 128), 1) < 64, values[0], values[1])

    pltpu.make_async_copy(row, g.at[idx], g_recv.at[0]).start()

    mine = lax.rem(idx, 4)

    def g_start(yy, zz, c):
        to = {"ent": zz * 16 + yy * 4 + lax.rem(mine + c, 4), "rep": rep}
        remote(row, g.at[idx], g_send.at[0], g_recv.at[0], to).start()

    def g_step(i, carry):
        for c in (2, 3, 1, 0):
            g_start(*far_first(i), c)
        return carry

    lax.fori_loop(0, 15, g_step, 0)
    for c in (2, 3, 1):
        g_start(y, z, c)
    order = order_ref[...]
    sub32 = lax.broadcasted_iota(jnp.int32, order.shape, 0)
    owner = order // 32
    inside = lax.rem(order // 16, 2) * 64 + lax.rem(order, 16)
    lane32 = lax.broadcasted_iota(jnp.int32, order.shape, 1)
    for n in range(2):
        pltpu.make_async_copy(whole[1 + n], whole[1 + n], r_send.at[1 + n]).wait()
    part = g.at[pl.ds(0, 63)]
    pltpu.make_async_copy(part, part, g_send.at[0]).wait()
    pltpu.make_async_copy(g, g, g_recv.at[0]).wait()

    picked = jnp.zeros(order.shape, F32)
    for i in range(64):
        picked = jnp.where(owner == i, g[i], picked)
    cols = []
    for m in range(4):
        col = jnp.sum(jnp.where(lane32 == inside + m * 16, picked, 0.0), axis=1, keepdims=True)
        cols.append(col)
    best = jnp.maximum(jnp.maximum(cols[0], cols[1]), jnp.maximum(cols[2], cols[3]))
    mean = sum(jnp.exp(c - best) for c in cols) * 0.25
    diagonal = sub32 == lane32
    out_ref[...] = jnp.zeros_like(out_ref)
    for m, col in enumerate(cols + [best + jnp.log(mean)]):
        out_ref[m : m + 1, :] = jnp.sum(jnp.where(diagonal, col, 0.0), axis=0, keepdims=True)


def build_kernel(
    head_ref, rel_ref, order_ref, tail_ref, ent_ref, table_ref, q_ref, tails_ref, wide_ref,
    head_rows, rel_rows, relf, head_at, sem,
):
    rows, width = ent_ref.shape[1:]
    half_width = width // 2
    offset = lax.axis_index("ent") * rows

    def fetch(i, carry):
        head = pl.multiple_of((head_ref[i] - offset) // 16 * 16, 16)
        pltpu.make_async_copy(ent_ref.at[:, pl.ds(head, 16)], head_rows.at[i], sem.at[0]).start()
        pltpu.make_async_copy(table_ref.at[rel_ref[i]], rel_rows.at[i], sem.at[1]).start()
        return carry

    lax.fori_loop(0, 32, fetch, 0, unroll=4)
    lane16 = lax.rem(lax.broadcasted_iota(jnp.int32, (1, 128), 1), 16)
    for k in range(2):
        acc = jnp.zeros((1, 128), jnp.int32)
        for i in range(16):
            acc = jnp.where(lane16 == i, tail_ref[k * 16 + i], acc)
        tails_ref[k] = acc
    for i in range(32):
        wide_ref[i : i + 1, :] = jnp.full((1, 128), order_ref[i], jnp.int32)
        head_at[i : i + 1, :] = jnp.full((1, 128), lax.rem(head_ref[i], 16), jnp.int32)
    pltpu.make_async_copy(rel_rows, rel_rows, sem.at[1]).wait()
    def spread(i, carry):
        right = rel_rows[i].astype(F32)
        for m in range(4):
            relf[m, pl.ds(i, 1), :] = right[m : m + 1, :]
        return carry

    lax.fori_loop(0, 32, spread, 0, unroll=8)
    pltpu.make_async_copy(head_rows, head_rows, sem.at[0]).wait()
    lane = lax.broadcasted_iota(jnp.int32, (32, 128), 1)
    sub = lax.broadcasted_iota(jnp.int32, (32, 128), 0)
    inside = lax.rem(lane, 16) == head_at[...]
    picker = jnp.concatenate(
        [jnp.where(jnp.logical_and(inside, lane // 16 + 8 * c == sub), 1.0, 0.0) for c in range(4)], axis=1
    ).astype(BF16)
    for m in range(4):
        left = jnp.dot(picker, head_rows[:, m].reshape(512, width), preferred_element_type=F32)
        a, b = left[:, :half_width], left[:, half_width:]
        c, d = relf[m, :, :half_width], relf[m, :, half_width:]
        q_ref[m, :, :half_width] = (a * c - b * d).astype(BF16)
        q_ref[m, :, half_width:] = (a * d + b * c).astype(BF16)


def split_kernel(out_ref, ens_ref, mem_ref):
    ens_ref[...] = out_ref[4:5, :32]
    mem_ref[...] = out_ref[0:4, :32]


def per_device(entity_table, relation_table, head_ids, relation_ids, order, tail_ids):
    members, local_count, width = entity_table.shape
    vmem = pl.BlockSpec(memory_space=pltpu.VMEM)
    smem = pl.BlockSpec(memory_space=pltpu.SMEM)
    hbm = pl.BlockSpec(memory_space=pl.ANY)
    dma = pltpu.SemaphoreType.DMA
    query, tails, order_wide = pl.pallas_call(
        build_kernel,
        out_shape=(
            jax.ShapeDtypeStruct((members, 32, width), BF16),
            jax.ShapeDtypeStruct((2, 1, 128), jnp.int32),
            jax.ShapeDtypeStruct((32, 128), jnp.int32),
        ),
        in_specs=[smem, smem, smem, smem, hbm, hbm],
        out_specs=(vmem, vmem, vmem),
        scratch_shapes=[
            pltpu.VMEM((32, members, 16, width), BF16),
            pltpu.VMEM((32, members, width), BF16),
            pltpu.VMEM((members, 32, width), F32),
            pltpu.VMEM((32, 128), jnp.int32),
            dma((2,)),
        ],
        compiler_params=pltpu.CompilerParams(vmem_limit_bytes=58 * 1024 * 1024),
        name="build_queries",
    )(head_ids, relation_ids, order, tail_ids, entity_table, jnp.transpose(relation_table, (1, 0, 2)))
    out = pl.pallas_call(
        score_kernel,
        out_shape=jax.ShapeDtypeStruct((8, 128), F32),
        in_specs=[vmem, vmem, vmem, hbm],
        out_specs=vmem,
        scratch_shapes=[
            pltpu.VMEM((4, 4, 4, 4, 16, width), BF16),
            pltpu.VMEM((2, 4, local_count, width), BF16),
            pltpu.VMEM((2 * local_count, 256), F32),
            pltpu.VMEM((2 * local_count, 256), F32),
            pltpu.VMEM((4, 4, 4, 1, 128), jnp.int32),
            pltpu.VMEM((4, 8, 256), jnp.int32),
            pltpu.VMEM((2, 4, 8, 128), F32),
            pltpu.VMEM((16, 4, 1, 128), F32),
            pltpu.VMEM((16, 4, 1, 128), F32),
            pltpu.VMEM((1, 128), F32),
            pltpu.VMEM((64, 1, 128), F32),
            dma((N_MSG,)),
            dma((N_MSG,)),
            dma((4,)),
            dma((4,)),
            dma((4,)),
            dma((3,)),
            dma((3,)),
            dma((1,)),
            dma((1,)),
        ],
        compiler_params=pltpu.CompilerParams(
            collective_id=0, has_side_effects=True, vmem_limit_bytes=58 * 1024 * 1024
        ),
        cost_estimate=pl.CostEstimate(
            flops=2 * members * 2048 * local_count * width,
            bytes_accessed=4 * members * local_count * width,
            transcendentals=members * 2048 * local_count,
        ),
        name="score_exchange",
    )(query, tails, order_wide, entity_table)
    ens, mem = pl.pallas_call(
        split_kernel,
        out_shape=(jax.ShapeDtypeStruct((1, 32), F32), jax.ShapeDtypeStruct((4, 32), F32)),
        in_specs=[vmem],
        out_specs=(vmem, vmem),
        name="split_output",
    )(out)
    return (ens.reshape(32), mem.T)


def solution(mesh):
    placed = (
        P(None, "ent", None),
        P(),
        P(("rep", "ent")),
        P(("rep", "ent")),
        P(("rep", "ent")),
        P(("rep", "ent")),
    )
    return jax.shard_map(
        per_device,
        mesh=mesh,
        in_specs=placed,
        out_specs=(P(("rep", "ent")), P(("rep", "ent"), None)),
        check_vma=False,
    )
```

```python
import jax
import jax.numpy as jnp
from jax import lax
from jax.experimental import pallas as pl
from jax.experimental.pallas import tpu as pltpu
from jax.sharding import PartitionSpec as P

MESH = pl.DeviceIdType.MESH
F32 = jnp.float32
BF16 = jnp.bfloat16

AXES = ("yz", "zy", "yz", "zy")
BATCH_M = (2, 3, 2, 3, 0, 1, 0, 1, 2, 2, 0, 1, 3, 3, 0, 1)
BATCH_K = (0, 0, 1, 1, 0, 0, 1, 1, 2, 3, 2, 2, 2, 3, 3, 3)
N_MSG = 160


def lookup(table, t):
    low = sum(v << (2 * i) for i, v in enumerate(table[:8]))
    high = sum(v << (2 * i) for i, v in enumerate(table[8:]))
    return (jnp.where(t < 8, low, high) >> (2 * lax.rem(t, 8))) & 3


def score_kernel(
    q_ref, tails_ref, order_ref, ent_ref, out_ref,
    u, e, s0, s1, tb, tv, stat, rowed, r, row, g,
    order_in, in_sem, send, recv, e_local, e_send, e_recv, r_send, r_recv, g_send, g_recv,
):
    rows, width = e.shape[2:]
    idx = lax.axis_index("ent")
    rep = lax.axis_index("rep")
    core = lax.rem(idx, 2)
    x_lo = lax.rem(idx // 2, 2)
    x = rep * 2 + x_lo
    y = lax.rem(idx // 4, 4)
    z = idx // 16
    src = y * 4 + z

    def dev(xx, yy, zz, cc):
        return {"ent": ((zz * 4 + yy) * 2 + lax.rem(xx, 2)) * 2 + cc, "rep": xx // 2}

    def wrap(v):
        return lax.rem(v + 4, 4)

    def along(axis, shift):
        if axis == "x":
            return dev(wrap(x + shift), y, z, core)
        return dev(x, wrap(y + shift), z, core) if axis == "y" else dev(x, y, wrap(z + shift), core)

    def remote(a, b, send_sem, recv_sem, to):
        return pltpu.make_async_remote_copy(
            src_ref=a, dst_ref=b, send_sem=send_sem, recv_sem=recv_sem, device_id=to, device_id_type=MESH
        )

    def e_own(m):
        return pltpu.make_async_copy(ent_ref.at[m], e.at[0, m], e_local.at[m])

    def e_copy(m):
        return remote(ent_ref.at[m], e.at[1, m], e_send.at[m], e_recv.at[m], dev(x, y, z, 1 - core))


    barrier = pltpu.get_barrier_semaphore()
    partners = [along(axis, shift) for axis in "xyz" for shift in (1, -1)] + [dev(x, y, z, 1 - core)]
    for partner in partners:
        pl.semaphore_signal(barrier, inc=1, device_id=partner, device_id_type=MESH)

    for m in (2, 3, 0, 1):
        for k in range(2):
            pltpu.make_async_copy(q_ref.at[m, pl.ds(16 * k, 16)], u.at[m, k, y, z], in_sem.at[m]).start()
    own_tails = tb.at[pl.ds(0, 2), y, z]
    pltpu.make_async_copy(tails_ref, own_tails, in_sem.at[4]).start()
    pltpu.make_async_copy(order_ref, order_in, in_sem.at[5]).start()
    for m in (2, 3, 0, 1):
        e_own(m).start()
    pl.semaphore_wait(barrier, len(partners))

    numbers = {}
    sent = {}

    def sem_of(key):
        return numbers.setdefault(key, len(numbers))

    def at(m, k, first, second):
        return u.at[m, k, first, second] if AXES[m][0] == "y" else u.at[m, k, second, first]

    def own(m, ph):
        return y if AXES[m][ph] == "y" else z

    def piece(m, q):
        return slice(None) if q is None else wrap(own(m, 0) + q)

    def ring(m, ph, k, q, j):
        offset, shift = ((0, 1), (0, -1), (-1, 1) if k % 2 == 0 else (1, -1))[j]
        pos = wrap(own(m, ph) + offset)
        ref = at(m, k, pos, own(m, 1)) if ph == 0 else at(m, k, piece(m, q), pos)
        n = sem_of((m, ph, k, q, j))
        return remote(ref, ref, send.at[n], recv.at[n], along(AXES[m][ph], shift))

    def cross(m, k, q, i):
        pos = wrap(own(m, 1) + i)
        n = sem_of((m, k, q, i))
        return remote(
            at(m, k, piece(m, q), pos), at(m, k + 2, piece(m, q), pos), send.at[n], recv.at[n],
            along("x", 1 if k == 0 else -1),
        )

    def tail_ring(ph, j):
        offset, shift = ((0, 1), (0, -1), (-1, 1))[j]
        ref = tb.at[pl.ds(0, 2), wrap(y + offset), z] if ph == 0 else tb.at[pl.ds(0, 2), :, wrap(z + offset)]
        n = sem_of(("tail", ph, j))
        return remote(ref, ref, send.at[n], recv.at[n], along("yz"[ph], shift))

    def tail_cross(k):
        n = sem_of(("tail", k))
        return remote(tb.at[k], tb.at[k + 2], send.at[n], recv.at[n], along("x", 1 if k == 0 else -1))

    def start(make, *args):
        make(*args).start()
        sent[(make, args)] = True

    def arrived(make, *args):
        make(*args).wait_recv()

    def ring_start(m, ph, k, q=None):
        start(ring, m, ph, k, q, 0)
        start(ring, m, ph, k, q, 1)

    def ring_fwd(m, ph, k, q=None):
        arrived(ring, m, ph, k, q, k % 2)
        start(ring, m, ph, k, q, 2)

    def ring_fin(m, ph, k, q=None):
        arrived(ring, m, ph, k, q, 1 - k % 2)
        arrived(ring, m, ph, k, q, 2)

    for m in (2, 3, 0, 1):
        pltpu.make_async_copy(q_ref.at[m], q_ref.at[m], in_sem.at[m]).wait()
        if m == 0:
            pltpu.make_async_copy(tails_ref, own_tails, in_sem.at[4]).wait()
            for j in range(2):
                start(tail_ring, 0, j)
        for k in range(2):
            ring_start(m, 0, k)
        for k in range(2):
            if m >= 2:
                ring_start(m, 1, k, 0)
            start(cross, m, k, 0, 0)
    for m in (2, 3, 0, 1):
        e_copy(m).start()

    def second(m, k, q):
        if m >= 2:
            ring_start(m, 1, k, q)
        start(cross, m, k, q, 0)

    for m in (2, 3, 0, 1):
        for k in range(2):
            ring_fwd(m, 0, k)
            second(m, k, -1 if k == 0 else 1)
        for k in range(2):
            arrived(ring, m, 0, k, None, 1 - k)
            second(m, k, 1 if k == 0 else -1)
    arrived(tail_ring, 0, 0)
    start(tail_ring, 0, 2)
    for m in (2, 3):
        for k in range(2):
            ring_fwd(m, 1, k, 0)
    for m in (2, 3, 0, 1):
        for k in range(2):
            arrived(ring, m, 0, k, None, 2)
            second(m, k, 2)
    arrived(tail_ring, 0, 1)
    arrived(tail_ring, 0, 2)
    for j in range(2):
        start(tail_ring, 1, j)
    for k in range(2):
        for m in (2, 3):
            ring_fwd(m, 1, k, -1)
            ring_fwd(m, 1, k, 1)
    arrived(tail_ring, 1, 0)
    start(tail_ring, 1, 2)
    for k in range(2):
        for m in (2, 3):
            ring_fwd(m, 1, k, 2)
            start(cross, m, k, None, -1 if k == 0 else 1)
    for m in (0, 1):
        ring_start(m, 1, 0)
    arrived(tail_ring, 1, 1)
    arrived(tail_ring, 1, 2)
    for k in range(2):
        start(tail_cross, k)

    def second_done(m, k):
        for q in (0, -1, 1, 2):
            ring_fin(m, 1, k, q)
        for i in (1 if k == 0 else -1, 2):
            start(cross, m, k, None, i)

    def crossed(m, k):
        for q in (0, -1, 1, 2):
            arrived(cross, m, k - 2, q, 0)
        if m >= 2:
            for i in (-1, 1, 2):
                arrived(cross, m, k - 2, None, i)
        else:
            ring_start(m, 1, k)

    def e_ready(m):
        e_own(m).wait()
        e_copy(m).wait_recv()

    def stat_copy(n, xx, yy, zz):
        ks = ((0, 2), (2, 1), (3, 1))[n]
        return remote(
            rowed.at[yy * 4 + zz, pl.ds(*ks)], r.at[src, pl.ds(*ks)], r_send.at[n], r_recv.at[n], dev(xx, yy, zz, core)
        )

    def pack(k):
        skew = lax.rem(
            lax.broadcasted_iota(jnp.int32, (8, 128), 1) // 16 - lax.broadcasted_iota(jnp.int32, (8, 128), 0) + 8, 8
        )
        for half in range(2):
            tile = stat[half, k]
            out = tile
            for d in range(1, 8):
                out = jnp.where(skew == d, pltpu.roll(pltpu.roll(tile, 8 - d, 0), 16 * d, 1), out)
            for i in range(8):
                rowed[half * 8 + i, k] = out[i : i + 1, :]

    def far_first(i):
        order = 2 + (1 << 2) + (3 << 4)
        return wrap(y + ((order >> (2 * (i // 4))) & 3)), wrap(z + ((order >> (2 * lax.rem(i, 4))) & 3))

    def send_all(n, xx, count):
        def step(i, carry):
            stat_copy(n, xx, *far_first(i)).start()
            return carry

        lax.fori_loop(0, count, step, 0)

    def comm(t):
        if t == 0:
            crossed(0, 2)
            crossed(1, 2)
            for m in (0, 1):
                ring_start(m, 1, 1)
            for k in range(2):
                for m in (2, 3):
                    second_done(m, k)
            e_ready(2)
        if t == 1:
            crossed(0, 3)
            crossed(1, 3)
            ring_fwd(0, 1, 0)
            ring_fwd(1, 1, 0)
            e_ready(3)
            for k in range(2):
                arrived(tail_cross, k)
            group = lax.broadcasted_iota(jnp.int32, (8, 128), 1) // 16
            for k in range(4):
                for half in range(2):
                    lanes = jnp.zeros((8, 128), jnp.int32)
                    for i in range(8):
                        lanes = jnp.where(group == i, tb[k, half * 2 + i // 4, i % 4], lanes)
                    tv[k, :, half * 128 : half * 128 + 128] = lanes
        if t == 2:
            ring_fwd(0, 1, 1)
            ring_fwd(1, 1, 1)
        if t == 4:
            e_ready(0)
            ring_fin(0, 1, 0)
        if t == 5:
            e_ready(1)
            ring_fin(1, 1, 0)
        if t == 6:
            ring_fwd(0, 1, 2)
            ring_fwd(1, 1, 2)
            ring_fin(0, 1, 1)
        if t == 7:
            ring_fin(1, 1, 1)
        if t == 8:
            crossed(2, 2)
        if t == 9:
            ring_fwd(0, 1, 3)
            ring_fwd(1, 1, 3)
            crossed(2, 3)
        if t == 10:
            pack(0)
            pack(1)
            pltpu.make_async_copy(rowed.at[src, pl.ds(0, 2)], r.at[src, pl.ds(0, 2)], r_recv.at[0]).start()
            send_all(0, x, 15)
            ring_fin(0, 1, 2)
        if t == 11:
            ring_fin(1, 1, 2)
        if t == 12:
            crossed(3, 2)
        if t == 13:
            crossed(3, 3)
        if t == 14:
            ring_fin(0, 1, 3)
        if t == 15:
            ring_fin(1, 1, 3)

    sub = lax.broadcasted_iota(jnp.int32, (8, 256), 0)
    blocks = rows // 8

    def dot(out, m, k):
        right = u[m, k].reshape(256, width)
        for j in range(2):
            out[j * rows : j * rows + rows, :] = lax.dot_general(
                e[j, m], right, (((1,), (1,)), ((), ())), preferred_element_type=F32
            )

    def process(ref, m, k):
        rel = [tv[k] - (idx + j * (1 - 2 * core)) * rows - sub for j in range(2)]
        tops = [ref[8 * i : 8 * i + 8, :] for i in range(4)]
        for i in range(4, 2 * blocks):
            tops[i % 4] = jnp.maximum(tops[i % 4], ref[8 * i : 8 * i + 8, :])
        top = jnp.maximum(jnp.maximum(tops[0], tops[1]), jnp.maximum(tops[2], tops[3]))
        top = jnp.max(top, axis=0, keepdims=True)
        wide = jnp.broadcast_to(top, (8, 256))
        sums = [jnp.zeros((8, 256), F32)] * 4
        true = [jnp.zeros((8, 256), F32)] * 2
        for i in range(2 * blocks):
            v = ref[8 * i : 8 * i + 8, :]
            sums[i % 4] = sums[i % 4] + jnp.exp(v - wide)
            j = i // blocks
            true[j] = jnp.where(rel[j] == 8 * (i % blocks), v, true[j])
        total = jnp.sum((sums[0] + sums[1]) + (sums[2] + sums[3]), axis=0, keepdims=True)
        lse = top + jnp.log(total)
        tail = jnp.sum(true[0] + true[1], axis=0, keepdims=True)
        for half in range(2):
            cols = slice(half * 128, half * 128 + 128)
            stat[half, k, pl.ds(m, 1), :] = lse[:, cols]
            stat[half, k, pl.ds(m + 4, 1), :] = tail[:, cols]

    s1[...] = jnp.zeros_like(s1)
    tv[...] = jnp.zeros_like(tv)

    def batches(i, carry):
        for p in range(2):
            t = 2 * i + p
            for j in range(p, 16, 2):
                pl.when(i == j // 2)(lambda j=j: comm(j))
            old = jnp.maximum(t - 1, 0)
            dot((s0, s1)[p], lookup(BATCH_M, t), lookup(BATCH_K, t))
            process((s1, s0)[p], lookup(BATCH_M, old), lookup(BATCH_K, old))
        return carry

    lax.fori_loop(0, 8, batches, 0)
    pack(2)
    send_all(1, wrap(x - 1), 16)
    process(s1, BATCH_M[15], BATCH_K[15])
    pack(3)
    send_all(2, wrap(x + 1), 16)

    whole = (r.at[:, pl.ds(0, 2)], r.at[:, pl.ds(2, 1)], r.at[:, pl.ds(3, 1)])
    part = r.at[pl.ds(0, 15), pl.ds(0, 2)]
    pltpu.make_async_copy(whole[0], whole[0], r_recv.at[0]).wait()
    pltpu.make_async_copy(part, part, r_send.at[0]).wait()

    def reduce(k):
        tiles = [r[i, k] for i in range(16)]
        top = tiles[0]
        total = tiles[0]
        for tile in tiles[1:]:
            top = jnp.maximum(top, tile)
            total = total + tile
        mass = jnp.exp(tiles[0] - top)
        for tile in tiles[1:]:
            mass = mass + jnp.exp(tile - top)
        return top, mass, total

    near = [reduce(0), reduce(1)]
    for copies in list(sent):
        make, args = copies
        make(*args).wait_send()
    for m in range(4):
        e_copy(m).wait_send()
    def half_turn(v):
        return pltpu.roll(jnp.broadcast_to(v, (8, 128)), 64, 1)[0:1, :]

    values = []
    for h in range(2):
        pltpu.make_async_copy(whole[1 + h], whole[1 + h], r_recv.at[1 + h]).wait()
        top0, mass0, total0 = near[h]
        top1, mass1, total1 = reduce(h + 2)
        top = jnp.maximum(top0, top1)
        lse = top + jnp.log(mass0 * jnp.exp(top0 - top) + mass1 * jnp.exp(top1 - top))
        total = total0 + total1
        values.append(half_turn(total) - lse if h == 0 else total - half_turn(lse))
    row[...] = jnp.where(lax.broadcasted_iota(jnp.int32, (1, 128), 1) < 64, values[0], values[1])

    pltpu.make_async_copy(row, g.at[idx], g_recv.at[0]).start()

    mine = lax.rem(idx, 4)

    def g_start(yy, zz, c):
        to = {"ent": zz * 16 + yy * 4 + lax.rem(mine + c, 4), "rep": rep}
        remote(row, g.at[idx], g_send.at[0], g_recv.at[0], to).start()

    def g_step(i, carry):
        for c in (2, 3, 1, 0):
            g_start(*far_first(i), c)
        return carry

    lax.fori_loop(0, 15, g_step, 0)
    for c in (2, 3, 1):
        g_start(y, z, c)
    pltpu.make_async_copy(order_ref, order_in, in_sem.at[5]).wait()
    order = order_in[...]
    sub32 = lax.broadcasted_iota(jnp.int32, order.shape, 0)
    owner = order // 32
    inside = lax.rem(order // 16, 2) * 64 + lax.rem(order, 16)
    lane32 = lax.broadcasted_iota(jnp.int32, order.shape, 1)
    for n in range(2):
        pltpu.make_async_copy(whole[1 + n], whole[1 + n], r_send.at[1 + n]).wait()
    part = g.at[pl.ds(0, 63)]
    pltpu.make_async_copy(part, part, g_send.at[0]).wait()
    pltpu.make_async_copy(g, g, g_recv.at[0]).wait()

    picked = jnp.zeros(order.shape, F32)
    for i in range(64):
        picked = jnp.where(owner == i, g[i], picked)
    cols = []
    for m in range(4):
        col = jnp.sum(jnp.where(lane32 == inside + m * 16, picked, 0.0), axis=1, keepdims=True)
        cols.append(col)
    best = jnp.maximum(jnp.maximum(cols[0], cols[1]), jnp.maximum(cols[2], cols[3]))
    mean = sum(jnp.exp(c - best) for c in cols) * 0.25
    diagonal = sub32 == lane32
    out_ref[...] = jnp.zeros_like(out_ref)
    for m, col in enumerate(cols + [best + jnp.log(mean)]):
        out_ref[m : m + 1, :] = jnp.sum(jnp.where(diagonal, col, 0.0), axis=0, keepdims=True)


def build_kernel(
    head_ref, rel_ref, order_ref, tail_ref, ent_ref, table_ref, q_ref, tails_ref, wide_ref,
    head_rows, rel_rows, relf, head_at, sem,
):
    rows, width = ent_ref.shape[1:]
    half_width = width // 2
    offset = lax.axis_index("ent") * rows

    def fetch(i, carry):
        head = pl.multiple_of((head_ref[i] - offset) // 16 * 16, 16)
        pltpu.make_async_copy(ent_ref.at[:, pl.ds(head, 16)], head_rows.at[i], sem.at[0]).start()
        pltpu.make_async_copy(table_ref.at[rel_ref[i]], rel_rows.at[i], sem.at[1]).start()
        return carry

    lax.fori_loop(0, 32, fetch, 0, unroll=4)
    lane16 = lax.rem(lax.broadcasted_iota(jnp.int32, (1, 128), 1), 16)
    for k in range(2):
        acc = jnp.zeros((1, 128), jnp.int32)
        for i in range(16):
            acc = jnp.where(lane16 == i, tail_ref[k * 16 + i], acc)
        tails_ref[k] = acc
    for i in range(32):
        wide_ref[i : i + 1, :] = jnp.full((1, 128), order_ref[i], jnp.int32)
        head_at[i : i + 1, :] = jnp.full((1, 128), lax.rem(head_ref[i], 16), jnp.int32)
    pltpu.make_async_copy(rel_rows, rel_rows, sem.at[1]).wait()
    def spread(i, carry):
        right = rel_rows[i].astype(F32)
        for m in range(4):
            relf[m, pl.ds(i, 1), :] = right[m : m + 1, :]
        return carry

    lax.fori_loop(0, 32, spread, 0, unroll=8)
    pltpu.make_async_copy(head_rows, head_rows, sem.at[0]).wait()
    lane = lax.broadcasted_iota(jnp.int32, (32, 128), 1)
    sub = lax.broadcasted_iota(jnp.int32, (32, 128), 0)
    inside = lax.rem(lane, 16) == head_at[...]
    picker = jnp.concatenate(
        [jnp.where(jnp.logical_and(inside, lane // 16 + 8 * c == sub), 1.0, 0.0) for c in range(4)], axis=1
    ).astype(BF16)
    for m in range(4):
        left = jnp.dot(picker, head_rows[:, m].reshape(512, width), preferred_element_type=F32)
        a, b = left[:, :half_width], left[:, half_width:]
        c, d = relf[m, :, :half_width], relf[m, :, half_width:]
        q_ref[m, :, :half_width] = (a * c - b * d).astype(BF16)
        q_ref[m, :, half_width:] = (a * d + b * c).astype(BF16)


def split_kernel(out_ref, ens_ref, mem_ref):
    ens_ref[...] = out_ref[4:5, :32]
    mem_ref[...] = out_ref[0:4, :32]


def per_device(entity_table, relation_table, head_ids, relation_ids, order, tail_ids):
    members, local_count, width = entity_table.shape
    vmem = pl.BlockSpec(memory_space=pltpu.VMEM)
    smem = pl.BlockSpec(memory_space=pltpu.SMEM)
    hbm = pl.BlockSpec(memory_space=pl.ANY)
    dma = pltpu.SemaphoreType.DMA
    query, tails, order_wide = pl.pallas_call(
        build_kernel,
        out_shape=(
            jax.ShapeDtypeStruct((members, 32, width), BF16),
            jax.ShapeDtypeStruct((2, 1, 128), jnp.int32),
            jax.ShapeDtypeStruct((32, 128), jnp.int32),
        ),
        in_specs=[smem, smem, smem, smem, hbm, hbm],
        out_specs=(vmem, vmem, vmem),
        scratch_shapes=[
            pltpu.VMEM((32, members, 16, width), BF16),
            pltpu.VMEM((32, members, width), BF16),
            pltpu.VMEM((members, 32, width), F32),
            pltpu.VMEM((32, 128), jnp.int32),
            dma((2,)),
        ],
        compiler_params=pltpu.CompilerParams(vmem_limit_bytes=58 * 1024 * 1024),
        name="build_queries",
    )(head_ids, relation_ids, order, tail_ids, entity_table, jnp.transpose(relation_table, (1, 0, 2)))
    out = pl.pallas_call(
        score_kernel,
        out_shape=jax.ShapeDtypeStruct((8, 128), F32),
        in_specs=[hbm, hbm, hbm, hbm],
        out_specs=vmem,
        scratch_shapes=[
            pltpu.VMEM((4, 4, 4, 4, 16, width), BF16),
            pltpu.VMEM((2, 4, local_count, width), BF16),
            pltpu.VMEM((2 * local_count, 256), F32),
            pltpu.VMEM((2 * local_count, 256), F32),
            pltpu.VMEM((4, 4, 4, 1, 128), jnp.int32),
            pltpu.VMEM((4, 8, 256), jnp.int32),
            pltpu.VMEM((2, 4, 8, 128), F32),
            pltpu.VMEM((16, 4, 1, 128), F32),
            pltpu.VMEM((16, 4, 1, 128), F32),
            pltpu.VMEM((1, 128), F32),
            pltpu.VMEM((64, 1, 128), F32),
            pltpu.VMEM((32, 128), jnp.int32),
            dma((6,)),
            dma((N_MSG,)),
            dma((N_MSG,)),
            dma((4,)),
            dma((4,)),
            dma((4,)),
            dma((3,)),
            dma((3,)),
            dma((1,)),
            dma((1,)),
        ],
        compiler_params=pltpu.CompilerParams(
            collective_id=0, has_side_effects=True, vmem_limit_bytes=58 * 1024 * 1024
        ),
        cost_estimate=pl.CostEstimate(
            flops=2 * members * 2048 * local_count * width,
            bytes_accessed=4 * members * local_count * width,
            transcendentals=members * 2048 * local_count,
        ),
        name="score_exchange",
    )(query, tails, order_wide, entity_table)
    ens, mem = pl.pallas_call(
        split_kernel,
        out_shape=(jax.ShapeDtypeStruct((1, 32), F32), jax.ShapeDtypeStruct((4, 32), F32)),
        in_specs=[vmem],
        out_specs=(vmem, vmem),
        name="split_output",
    )(out)
    return (ens.reshape(32), mem.T)


def solution(mesh):
    placed = (
        P(None, "ent", None),
        P(),
        P(("rep", "ent")),
        P(("rep", "ent")),
        P(("rep", "ent")),
        P(("rep", "ent")),
    )
    return jax.shard_map(
        per_device,
        mesh=mesh,
        in_specs=placed,
        out_specs=(P(("rep", "ent")), P(("rep", "ent"), None)),
        check_vma=False,
    )
```

```python
import jax
import jax.numpy as jnp
from jax import lax
from jax.experimental import pallas as pl
from jax.experimental.pallas import tpu as pltpu
from jax.sharding import PartitionSpec as P

MESH = pl.DeviceIdType.MESH
F32 = jnp.float32
BF16 = jnp.bfloat16

AXES = ("yz", "zy", "yz", "zy")
BATCH_M = (2, 3, 2, 3, 0, 1, 0, 1, 2, 2, 0, 1, 3, 3, 0, 1)
BATCH_K = (0, 0, 1, 1, 0, 0, 1, 1, 2, 3, 2, 2, 2, 3, 3, 3)
N_MSG = 160


def lookup(table, t):
    low = sum(v << (2 * i) for i, v in enumerate(table[:8]))
    high = sum(v << (2 * i) for i, v in enumerate(table[8:]))
    return (jnp.where(t < 8, low, high) >> (2 * lax.rem(t, 8))) & 3


def score_kernel(
    q_ref, tails_ref, order_ref, ent_ref, out_ref,
    u, e, s0, s1, tb, tv, stat, rowed, r, row, g,
    order_in, in_sem, send, recv, e_local, e_send, e_recv, r_send, r_recv, g_send, g_recv,
):
    rows, width = e.shape[2:]
    idx = lax.axis_index("ent")
    rep = lax.axis_index("rep")
    core = lax.rem(idx, 2)
    x_lo = lax.rem(idx // 2, 2)
    x = rep * 2 + x_lo
    y = lax.rem(idx // 4, 4)
    z = idx // 16
    src = y * 4 + z

    def dev(xx, yy, zz, cc):
        return {"ent": ((zz * 4 + yy) * 2 + lax.rem(xx, 2)) * 2 + cc, "rep": xx // 2}

    def wrap(v):
        return lax.rem(v + 4, 4)

    def along(axis, shift):
        if axis == "x":
            return dev(wrap(x + shift), y, z, core)
        return dev(x, wrap(y + shift), z, core) if axis == "y" else dev(x, y, wrap(z + shift), core)

    def remote(a, b, send_sem, recv_sem, to):
        return pltpu.make_async_remote_copy(
            src_ref=a, dst_ref=b, send_sem=send_sem, recv_sem=recv_sem, device_id=to, device_id_type=MESH
        )

    def e_own(m):
        return pltpu.make_async_copy(ent_ref.at[m], e.at[0, m], e_local.at[m])

    def e_copy(m):
        return remote(ent_ref.at[m], e.at[1, m], e_send.at[m], e_recv.at[m], dev(x, y, z, 1 - core))


    barrier = pltpu.get_barrier_semaphore()
    partners = [along(axis, shift) for axis in "xyz" for shift in (1, -1)] + [dev(x, y, z, 1 - core)]
    for partner in partners:
        pl.semaphore_signal(barrier, inc=1, device_id=partner, device_id_type=MESH)

    for m in (2, 3, 0, 1):
        for k in range(2):
            pltpu.make_async_copy(q_ref.at[m, pl.ds(16 * k, 16)], u.at[m, k, y, z], in_sem.at[m]).start()
    own_tails = tb.at[pl.ds(0, 2), y, z]
    pltpu.make_async_copy(tails_ref, own_tails, in_sem.at[4]).start()
    pltpu.make_async_copy(order_ref, order_in, in_sem.at[5]).start()
    for m in (2, 3, 0, 1):
        e_own(m).start()
    pl.semaphore_wait(barrier, len(partners))

    numbers = {}
    sent = {}

    def sem_of(key):
        return numbers.setdefault(key, len(numbers))

    def at(m, k, first, second):
        return u.at[m, k, first, second] if AXES[m][0] == "y" else u.at[m, k, second, first]

    def own(m, ph):
        return y if AXES[m][ph] == "y" else z

    def piece(m, q):
        return slice(None) if q is None else wrap(own(m, 0) + q)

    def ring(m, ph, k, q, j):
        offset, shift = ((0, 1), (0, -1), (-1, 1) if k % 2 == 0 else (1, -1))[j]
        pos = wrap(own(m, ph) + offset)
        ref = at(m, k, pos, own(m, 1)) if ph == 0 else at(m, k, piece(m, q), pos)
        n = sem_of((m, ph, k, q, j))
        return remote(ref, ref, send.at[n], recv.at[n], along(AXES[m][ph], shift))

    def cross(m, k, q, i):
        pos = wrap(own(m, 1) + i)
        n = sem_of((m, k, q, i))
        return remote(
            at(m, k, piece(m, q), pos), at(m, k + 2, piece(m, q), pos), send.at[n], recv.at[n],
            along("x", 1 if k == 0 else -1),
        )

    def tail_ring(ph, j):
        offset, shift = ((0, 1), (0, -1), (-1, 1))[j]
        ref = tb.at[pl.ds(0, 2), wrap(y + offset), z] if ph == 0 else tb.at[pl.ds(0, 2), :, wrap(z + offset)]
        n = sem_of(("tail", ph, j))
        return remote(ref, ref, send.at[n], recv.at[n], along("yz"[ph], shift))

    def tail_cross(k):
        n = sem_of(("tail", k))
        return remote(tb.at[k], tb.at[k + 2], send.at[n], recv.at[n], along("x", 1 if k == 0 else -1))

    def start(make, *args):
        make(*args).start()
        sent[(make, args)] = True

    def arrived(make, *args):
        make(*args).wait_recv()

    def ring_start(m, ph, k, q=None):
        start(ring, m, ph, k, q, 0)
        start(ring, m, ph, k, q, 1)

    def ring_fwd(m, ph, k, q=None):
        arrived(ring, m, ph, k, q, k % 2)
        start(ring, m, ph, k, q, 2)

    def ring_fin(m, ph, k, q=None):
        arrived(ring, m, ph, k, q, 1 - k % 2)
        arrived(ring, m, ph, k, q, 2)

    for m in (2, 3, 0, 1):
        pltpu.make_async_copy(q_ref.at[m], q_ref.at[m], in_sem.at[m]).wait()
        if m == 0:
            pltpu.make_async_copy(tails_ref, own_tails, in_sem.at[4]).wait()
            for j in range(2):
                start(tail_ring, 0, j)
        for k in range(2):
            ring_start(m, 0, k)
        for k in range(2):
            if m >= 2:
                ring_start(m, 1, k, 0)
            start(cross, m, k, 0, 0)
    for m in (2, 3, 0, 1):
        e_copy(m).start()

    def second(m, k, q):
        if m >= 2:
            ring_start(m, 1, k, q)
        start(cross, m, k, q, 0)

    for m in (2, 3, 0, 1):
        for k in range(2):
            ring_fwd(m, 0, k)
            second(m, k, -1 if k == 0 else 1)
        for k in range(2):
            arrived(ring, m, 0, k, None, 1 - k)
            second(m, k, 1 if k == 0 else -1)
    arrived(tail_ring, 0, 0)
    start(tail_ring, 0, 2)
    for m in (2, 3):
        for k in range(2):
            ring_fwd(m, 1, k, 0)
    for m in (2, 3, 0, 1):
        for k in range(2):
            arrived(ring, m, 0, k, None, 2)
            second(m, k, 2)
    arrived(tail_ring, 0, 1)
    arrived(tail_ring, 0, 2)
    for j in range(2):
        start(tail_ring, 1, j)
    for k in range(2):
        for m in (2, 3):
            ring_fwd(m, 1, k, -1)
            ring_fwd(m, 1, k, 1)
    arrived(tail_ring, 1, 0)
    start(tail_ring, 1, 2)
    for k in range(2):
        for m in (2, 3):
            ring_fwd(m, 1, k, 2)
            start(cross, m, k, None, -1 if k == 0 else 1)
    for m in (0, 1):
        ring_start(m, 1, 0)
    arrived(tail_ring, 1, 1)
    arrived(tail_ring, 1, 2)
    for k in range(2):
        start(tail_cross, k)

    def second_done(m, k):
        for q in (0, -1, 1, 2):
            ring_fin(m, 1, k, q)
        for i in (1 if k == 0 else -1, 2):
            start(cross, m, k, None, i)

    def crossed(m, k):
        for q in (0, -1, 1, 2):
            arrived(cross, m, k - 2, q, 0)
        if m >= 2:
            for i in (-1, 1, 2):
                arrived(cross, m, k - 2, None, i)
        else:
            ring_start(m, 1, k)

    def e_ready(m):
        e_own(m).wait()
        e_copy(m).wait_recv()

    def stat_copy(n, xx, yy, zz):
        ks = ((0, 2), (2, 1), (3, 1))[n]
        return remote(
            rowed.at[yy * 4 + zz, pl.ds(*ks)], r.at[src, pl.ds(*ks)], r_send.at[n], r_recv.at[n], dev(xx, yy, zz, core)
        )

    def pack(k):
        skew = lax.rem(
            lax.broadcasted_iota(jnp.int32, (8, 128), 1) // 16 - lax.broadcasted_iota(jnp.int32, (8, 128), 0) + 8, 8
        )
        for half in range(2):
            tile = stat[half, k]
            out = tile
            for d in range(1, 8):
                out = jnp.where(skew == d, pltpu.roll(pltpu.roll(tile, 8 - d, 0), 16 * d, 1), out)
            for i in range(8):
                rowed[half * 8 + i, k] = out[i : i + 1, :]

    def far_first(i):
        order = 2 + (1 << 2) + (3 << 4)
        return wrap(y + ((order >> (2 * (i // 4))) & 3)), wrap(z + ((order >> (2 * lax.rem(i, 4))) & 3))

    def send_all(n, xx, count):
        def step(i, carry):
            stat_copy(n, xx, *far_first(i)).start()
            return carry

        lax.fori_loop(0, count, step, 0)

    def comm(t):
        if t == 0:
            crossed(0, 2)
            crossed(1, 2)
            for m in (0, 1):
                ring_start(m, 1, 1)
            for k in range(2):
                for m in (2, 3):
                    second_done(m, k)
            e_ready(2)
        if t == 1:
            crossed(0, 3)
            crossed(1, 3)
            ring_fwd(0, 1, 0)
            ring_fwd(1, 1, 0)
            e_ready(3)
            for k in range(2):
                arrived(tail_cross, k)
            group = lax.broadcasted_iota(jnp.int32, (8, 128), 1) // 16
            for k in range(4):
                for half in range(2):
                    lanes = jnp.zeros((8, 128), jnp.int32)
                    for i in range(8):
                        lanes = jnp.where(group == i, tb[k, half * 2 + i // 4, i % 4], lanes)
                    tv[k, :, half * 128 : half * 128 + 128] = lanes
        if t == 2:
            ring_fwd(0, 1, 1)
            ring_fwd(1, 1, 1)
        if t == 4:
            e_ready(0)
            ring_fin(0, 1, 0)
        if t == 5:
            e_ready(1)
            ring_fin(1, 1, 0)
        if t == 6:
            ring_fwd(0, 1, 2)
            ring_fwd(1, 1, 2)
            ring_fin(0, 1, 1)
        if t == 7:
            ring_fin(1, 1, 1)
        if t == 8:
            crossed(2, 2)
        if t == 9:
            pack(0)
            pack(1)
            pltpu.make_async_copy(rowed.at[src, pl.ds(0, 2)], r.at[src, pl.ds(0, 2)], r_recv.at[0]).start()
            send_all(0, x, 15)
            ring_fwd(0, 1, 3)
            ring_fwd(1, 1, 3)
            crossed(2, 3)
        if t == 10:
            ring_fin(0, 1, 2)
        if t == 11:
            ring_fin(1, 1, 2)
        if t == 12:
            crossed(3, 2)
        if t == 13:
            crossed(3, 3)
        if t == 14:
            ring_fin(0, 1, 3)
        if t == 15:
            ring_fin(1, 1, 3)

    sub = lax.broadcasted_iota(jnp.int32, (8, 256), 0)
    blocks = rows // 8

    def dot(out, m, k):
        right = u[m, k].reshape(256, width)
        for j in range(2):
            out[j * rows : j * rows + rows, :] = lax.dot_general(
                e[j, m], right, (((1,), (1,)), ((), ())), preferred_element_type=F32
            )

    def process(ref, m, k):
        rel = [tv[k] - (idx + j * (1 - 2 * core)) * rows - sub for j in range(2)]
        tops = [ref[8 * i : 8 * i + 8, :] for i in range(4)]
        for i in range(4, 2 * blocks):
            tops[i % 4] = jnp.maximum(tops[i % 4], ref[8 * i : 8 * i + 8, :])
        top = jnp.maximum(jnp.maximum(tops[0], tops[1]), jnp.maximum(tops[2], tops[3]))
        top = jnp.max(top, axis=0, keepdims=True)
        wide = jnp.broadcast_to(top, (8, 256))
        sums = [jnp.zeros((8, 256), F32)] * 4
        true = [jnp.zeros((8, 256), F32)] * 2
        for i in range(2 * blocks):
            v = ref[8 * i : 8 * i + 8, :]
            sums[i % 4] = sums[i % 4] + jnp.exp(v - wide)
            j = i // blocks
            true[j] = jnp.where(rel[j] == 8 * (i % blocks), v, true[j])
        total = jnp.sum((sums[0] + sums[1]) + (sums[2] + sums[3]), axis=0, keepdims=True)
        lse = top + jnp.log(total)
        tail = jnp.sum(true[0] + true[1], axis=0, keepdims=True)
        for half in range(2):
            cols = slice(half * 128, half * 128 + 128)
            stat[half, k, pl.ds(m, 1), :] = lse[:, cols]
            stat[half, k, pl.ds(m + 4, 1), :] = tail[:, cols]

    s1[...] = jnp.zeros_like(s1)
    tv[...] = jnp.zeros_like(tv)

    def batches(i, carry):
        for p in range(2):
            t = 2 * i + p
            for j in range(p, 16, 2):
                pl.when(i == j // 2)(lambda j=j: comm(j))
            old = jnp.maximum(t - 1, 0)
            dot((s0, s1)[p], lookup(BATCH_M, t), lookup(BATCH_K, t))
            process((s1, s0)[p], lookup(BATCH_M, old), lookup(BATCH_K, old))
        return carry

    lax.fori_loop(0, 8, batches, 0)
    pack(2)
    send_all(1, wrap(x - 1), 16)
    process(s1, BATCH_M[15], BATCH_K[15])
    pack(3)
    send_all(2, wrap(x + 1), 16)

    whole = (r.at[:, pl.ds(0, 2)], r.at[:, pl.ds(2, 1)], r.at[:, pl.ds(3, 1)])
    part = r.at[pl.ds(0, 15), pl.ds(0, 2)]
    pltpu.make_async_copy(whole[0], whole[0], r_recv.at[0]).wait()
    pltpu.make_async_copy(part, part, r_send.at[0]).wait()

    def reduce(k):
        tiles = [r[i, k] for i in range(16)]
        top = tiles[0]
        total = tiles[0]
        for tile in tiles[1:]:
            top = jnp.maximum(top, tile)
            total = total + tile
        mass = jnp.exp(tiles[0] - top)
        for tile in tiles[1:]:
            mass = mass + jnp.exp(tile - top)
        return top, mass, total

    near = [reduce(0), reduce(1)]
    for copies in list(sent):
        make, args = copies
        make(*args).wait_send()
    for m in range(4):
        e_copy(m).wait_send()
    def half_turn(v):
        return pltpu.roll(jnp.broadcast_to(v, (8, 128)), 64, 1)[0:1, :]

    values = []
    for h in range(2):
        pltpu.make_async_copy(whole[1 + h], whole[1 + h], r_recv.at[1 + h]).wait()
        top0, mass0, total0 = near[h]
        top1, mass1, total1 = reduce(h + 2)
        top = jnp.maximum(top0, top1)
        lse = top + jnp.log(mass0 * jnp.exp(top0 - top) + mass1 * jnp.exp(top1 - top))
        total = total0 + total1
        values.append(half_turn(total) - lse if h == 0 else total - half_turn(lse))
    row[...] = jnp.where(lax.broadcasted_iota(jnp.int32, (1, 128), 1) < 64, values[0], values[1])

    pltpu.make_async_copy(row, g.at[idx], g_recv.at[0]).start()

    mine = lax.rem(idx, 4)

    def g_start(yy, zz, c):
        to = {"ent": zz * 16 + yy * 4 + lax.rem(mine + c, 4), "rep": rep}
        remote(row, g.at[idx], g_send.at[0], g_recv.at[0], to).start()

    def g_step(i, carry):
        for c in (2, 3, 1, 0):
            g_start(*far_first(i), c)
        return carry

    lax.fori_loop(0, 15, g_step, 0)
    for c in (2, 3, 1):
        g_start(y, z, c)
    pltpu.make_async_copy(order_ref, order_in, in_sem.at[5]).wait()
    order = order_in[...]
    sub32 = lax.broadcasted_iota(jnp.int32, order.shape, 0)
    owner = order // 32
    inside = lax.rem(order // 16, 2) * 64 + lax.rem(order, 16)
    lane32 = lax.broadcasted_iota(jnp.int32, order.shape, 1)
    for n in range(2):
        pltpu.make_async_copy(whole[1 + n], whole[1 + n], r_send.at[1 + n]).wait()
    part = g.at[pl.ds(0, 63)]
    pltpu.make_async_copy(part, part, g_send.at[0]).wait()
    pltpu.make_async_copy(g, g, g_recv.at[0]).wait()

    picked = jnp.zeros(order.shape, F32)
    for i in range(64):
        picked = jnp.where(owner == i, g[i], picked)
    cols = []
    for m in range(4):
        col = jnp.sum(jnp.where(lane32 == inside + m * 16, picked, 0.0), axis=1, keepdims=True)
        cols.append(col)
    best = jnp.maximum(jnp.maximum(cols[0], cols[1]), jnp.maximum(cols[2], cols[3]))
    mean = sum(jnp.exp(c - best) for c in cols) * 0.25
    diagonal = sub32 == lane32
    out_ref[...] = jnp.zeros_like(out_ref)
    for m, col in enumerate(cols + [best + jnp.log(mean)]):
        out_ref[m : m + 1, :] = jnp.sum(jnp.where(diagonal, col, 0.0), axis=0, keepdims=True)


def build_kernel(
    head_ref, rel_ref, order_ref, tail_ref, ent_ref, table_ref, q_ref, tails_ref, wide_ref,
    head_rows, rel_rows, relf, head_at, sem,
):
    rows, width = ent_ref.shape[1:]
    half_width = width // 2
    offset = lax.axis_index("ent") * rows

    def fetch(i, carry):
        head = pl.multiple_of((head_ref[i] - offset) // 16 * 16, 16)
        pltpu.make_async_copy(ent_ref.at[:, pl.ds(head, 16)], head_rows.at[i], sem.at[0]).start()
        pltpu.make_async_copy(table_ref.at[rel_ref[i]], rel_rows.at[i], sem.at[1]).start()
        return carry

    lax.fori_loop(0, 32, fetch, 0, unroll=16)
    lane16 = lax.rem(lax.broadcasted_iota(jnp.int32, (1, 128), 1), 16)
    for k in range(2):
        acc = jnp.zeros((1, 128), jnp.int32)
        for i in range(16):
            acc = jnp.where(lane16 == i, tail_ref[k * 16 + i], acc)
        tails_ref[k] = acc
    for i in range(32):
        wide_ref[i : i + 1, :] = jnp.full((1, 128), order_ref[i], jnp.int32)
        head_at[i : i + 1, :] = jnp.full((1, 128), lax.rem(head_ref[i], 16), jnp.int32)
    pltpu.make_async_copy(rel_rows, rel_rows, sem.at[1]).wait()
    def spread(i, carry):
        right = rel_rows[i].astype(F32)
        for m in range(4):
            relf[m, pl.ds(i, 1), :] = right[m : m + 1, :]
        return carry

    lax.fori_loop(0, 32, spread, 0, unroll=8)
    pltpu.make_async_copy(head_rows, head_rows, sem.at[0]).wait()
    lane = lax.broadcasted_iota(jnp.int32, (32, 128), 1)
    sub = lax.broadcasted_iota(jnp.int32, (32, 128), 0)
    inside = lax.rem(lane, 16) == head_at[...]
    picker = jnp.concatenate(
        [jnp.where(jnp.logical_and(inside, lane // 16 + 8 * c == sub), 1.0, 0.0) for c in range(4)], axis=1
    ).astype(BF16)
    for m in range(4):
        left = jnp.dot(picker, head_rows[:, m].reshape(512, width), preferred_element_type=F32)
        a, b = left[:, :half_width], left[:, half_width:]
        c, d = relf[m, :, :half_width], relf[m, :, half_width:]
        q_ref[m, :, :half_width] = (a * c - b * d).astype(BF16)
        q_ref[m, :, half_width:] = (a * d + b * c).astype(BF16)


def split_kernel(out_ref, ens_ref, mem_ref):
    ens_ref[...] = out_ref[4:5, :32]
    mem_ref[...] = out_ref[0:4, :32]


def per_device(entity_table, relation_table, head_ids, relation_ids, order, tail_ids):
    members, local_count, width = entity_table.shape
    vmem = pl.BlockSpec(memory_space=pltpu.VMEM)
    smem = pl.BlockSpec(memory_space=pltpu.SMEM)
    hbm = pl.BlockSpec(memory_space=pl.ANY)
    dma = pltpu.SemaphoreType.DMA
    query, tails, order_wide = pl.pallas_call(
        build_kernel,
        out_shape=(
            jax.ShapeDtypeStruct((members, 32, width), BF16),
            jax.ShapeDtypeStruct((2, 1, 128), jnp.int32),
            jax.ShapeDtypeStruct((32, 128), jnp.int32),
        ),
        in_specs=[smem, smem, smem, smem, hbm, hbm],
        out_specs=(vmem, vmem, vmem),
        scratch_shapes=[
            pltpu.VMEM((32, members, 16, width), BF16),
            pltpu.VMEM((32, members, width), BF16),
            pltpu.VMEM((members, 32, width), F32),
            pltpu.VMEM((32, 128), jnp.int32),
            dma((2,)),
        ],
        compiler_params=pltpu.CompilerParams(vmem_limit_bytes=58 * 1024 * 1024),
        name="build_queries",
    )(head_ids, relation_ids, order, tail_ids, entity_table, jnp.transpose(relation_table, (1, 0, 2)))
    out = pl.pallas_call(
        score_kernel,
        out_shape=jax.ShapeDtypeStruct((8, 128), F32),
        in_specs=[hbm, hbm, hbm, hbm],
        out_specs=vmem,
        scratch_shapes=[
            pltpu.VMEM((4, 4, 4, 4, 16, width), BF16),
            pltpu.VMEM((2, 4, local_count, width), BF16),
            pltpu.VMEM((2 * local_count, 256), F32),
            pltpu.VMEM((2 * local_count, 256), F32),
            pltpu.VMEM((4, 4, 4, 1, 128), jnp.int32),
            pltpu.VMEM((4, 8, 256), jnp.int32),
            pltpu.VMEM((2, 4, 8, 128), F32),
            pltpu.VMEM((16, 4, 1, 128), F32),
            pltpu.VMEM((16, 4, 1, 128), F32),
            pltpu.VMEM((1, 128), F32),
            pltpu.VMEM((64, 1, 128), F32),
            pltpu.VMEM((32, 128), jnp.int32),
            dma((6,)),
            dma((N_MSG,)),
            dma((N_MSG,)),
            dma((4,)),
            dma((4,)),
            dma((4,)),
            dma((3,)),
            dma((3,)),
            dma((1,)),
            dma((1,)),
        ],
        compiler_params=pltpu.CompilerParams(
            collective_id=0, has_side_effects=True, vmem_limit_bytes=58 * 1024 * 1024
        ),
        cost_estimate=pl.CostEstimate(
            flops=2 * members * 2048 * local_count * width,
            bytes_accessed=4 * members * local_count * width,
            transcendentals=members * 2048 * local_count,
        ),
        name="score_exchange",
    )(query, tails, order_wide, entity_table)
    ens, mem = pl.pallas_call(
        split_kernel,
        out_shape=(jax.ShapeDtypeStruct((1, 32), F32), jax.ShapeDtypeStruct((4, 32), F32)),
        in_specs=[vmem],
        out_specs=(vmem, vmem),
        name="split_output",
    )(out)
    return (ens.reshape(32), mem.T)


def solution(mesh):
    placed = (
        P(None, "ent", None),
        P(),
        P(("rep", "ent")),
        P(("rep", "ent")),
        P(("rep", "ent")),
        P(("rep", "ent")),
    )
    return jax.shard_map(
        per_device,
        mesh=mesh,
        in_specs=placed,
        out_specs=(P(("rep", "ent")), P(("rep", "ent"), None)),
        check_vma=False,
    )
```
